32 devices in a mesh: groups: 2 (over x), loop: 16 (over z, y, core).
Axes of the slice: x: 2, y: 2, z: 4, core: 2. Of those that a mesh axis runs over, the one named last changes fastest.
Arguments:
- activations: bfloat16 [5120, 4096], P('loop', 'groups'), parts along dimension 1, may hold values from -6 to 6
- out_grads: bfloat16 [20480, 4096], P('loop', 'groups'), parts along dimension 1, may hold values from -6 to 6
- left_factors: bfloat16 [256, 5120], P('loop'), may hold values from -0.078125 to 0.078125
- right_factors: bfloat16 [256, 20480], P('loop'), may hold values from -0.0390625 to 0.0390625
- token_ids: int32 [4096], P(('groups', 'loop')), parts along dimension 0, may hold values from 0 to 50687
- doc_starts: int32 [4096], P(('groups', 'loop')), parts along dimension 0, may hold values 0 or 1
- token_weights: float32 [50688], replicated, may hold values from 0.25 to 4
Outputs:
- scores: float32 [4096, 8], P(('groups', 'loop')), parts along dimension 0
- doc_influence: float32 [4096, 8], P(('groups', 'loop')), parts along dimension 0
The draws below stay inside these ranges and needn't reach their ends.
There are 2 independent parts, one for each index of `groups`. The reference program is written for one: setup_inputs(seed, part) draws one part's arguments, and reference() takes and returns one part's arrays. A program takes and returns all parts, laid end to end along the dimension named above; an argument that names none is the same for every part. Nothing has to cross between parts.
All inputs are finite; a program needn't handle non-finite values. No bound on the sum of `doc_starts` on one device may be relied on, other than what follows from the above.
Results may differ from the reference program's by a relative error of at most 0.0003.
Values may be sent and summed in bfloat16 or wider, within the bound.
No kernel may reach another device: no remote copies, remote signals or barrier semaphores. Data moves between devices by JAX's collectives and lax.ppermute only.
A program may use at most 128 MiB of HBM per device.

```python
import math
import jax
import jax.numpy as jnp
import numpy as np
from jax import lax

D = 5120
FF = 20480
VOCAB = 50688
TOK_DEV = 128
QUERIES = 8
RANK = 32
TOKENS = 2048
FACTORS = 256


def set_ends(values, rng, smallest, high):
    shape = values.shape
    spot = [jax.random.randint(jax.random.fold_in(rng, axis), (), 0, shape[axis]) for axis in range(len(shape))]
    values = values.at[tuple(spot)].set(smallest)
    longest = shape.index(max(shape))
    spot[longest] = (spot[longest] + 1) % shape[longest]
    return values.at[tuple(spot)].set(high)


def level_of(key, shape, cuts, low, largest):
    def one(dim, blocks):
        heights = jax.random.uniform(jax.random.fold_in(jax.random.fold_in(key, 6), dim), (blocks,), jnp.float32, low / len(cuts), largest / len(cuts))
        return jnp.repeat(jnp.exp(heights), shape[dim] // blocks).reshape((-1,) + (1,) * (len(shape) - dim - 1))

    gain = one(*cuts[0])
    for cut in cuts[1:]:
        gain = gain * one(*cut)
    return gain


def cumulative_ranks(count, skew):
    portions = [(1 << 20) // math.isqrt(rank ** skew) + 1 for rank in range(1, count + 1)]
    scale = 1 + sum(portions) // (1 << 30)
    return np.cumsum(np.array([max(1, weight // scale) for weight in portions]))


def ranked(stream_key, dims, amount, skew):
    grid = cumulative_ranks(amount, skew)
    lot = jax.random.randint(jax.random.fold_in(stream_key, 1), dims, 0, int(grid[amount - 1]))
    rank = jnp.searchsorted(jnp.asarray(grid, jnp.int32), lot, side="right")
    return jax.random.permutation(jax.random.fold_in(stream_key, 2), amount)[rank].astype(jnp.int32)


def noise(stream_key, shape, scale, most, cuts=(), kind=jnp.bfloat16):
    loudness = level_of(stream_key, shape, cuts, -0.22, 0.18) if cuts else 1.0
    entries = jax.random.normal(stream_key, shape, jnp.float32) * scale * loudness
    return jnp.minimum(jnp.maximum(entries, -most), most).astype(kind)


def setup_inputs(seed: int = 0, part: int = 0) -> dict:
    splits = jax.random.split(jax.random.key(seed), 8)
    part_splits = jax.random.split(jax.random.fold_in(splits[7], part), 8)
    return {
        "activations": noise(part_splits[0], (D, TOKENS), 1.0, 6.0, ((0, 16),)),
        "out_grads": noise(part_splits[1], (FF, TOKENS), 1.0, 6.0, ((0, 16),)),
        "left_factors": noise(splits[2], (FACTORS, D), D ** -0.5, 0.078125, ((0, 16),)),
        "right_factors": noise(splits[3], (FACTORS, FF), FF ** -0.5, 0.0390625, ((0, 16),)),
        "token_ids": set_ends(ranked(part_splits[4], (TOKENS,), VOCAB, 2), jax.random.fold_in(part_splits[4], 3), 0, VOCAB - 1).astype(jnp.int32),
        "doc_starts": set_ends((jax.random.randint(part_splits[5], (TOKENS,), 0, 32 * TOK_DEV) < 1).astype(jnp.int32), jax.random.fold_in(part_splits[5], 1), 0, 1),
        "token_weights": jnp.clip(jnp.exp(jax.random.uniform(splits[6], (VOCAB,), jnp.float32, math.log(0.25), math.log(4.0))), 0.25, 4.0),
    }


def merge_docs(earlier, later):
    taken = later[2] > 0
    return (jnp.where(taken[:, None], later[0], earlier[0] + later[0]), jnp.where(taken, later[1], earlier[1] + later[1]), jnp.maximum(earlier[2], later[2]))

def reference(activations, out_grads, left_factors, right_factors, token_ids, doc_starts, token_weights):
    left_proj = lax.dot_general(activations, left_factors, (((0,), (1,)), ((), ())), preferred_element_type=jnp.float32)
    right_proj = lax.dot_general(out_grads, right_factors, (((0,), (1,)), ((), ())), preferred_element_type=jnp.float32)
    products = (left_proj * right_proj).reshape(TOKENS, QUERIES, RANK).sum(axis=-1)
    weights = jnp.take(token_weights, token_ids)
    scores = products * (weights * RANK ** (-0.5))[:, None]
    flags = doc_starts.astype(jnp.float32)
    unit_counts = jnp.ones((TOKENS,), jnp.float32)
    doc_sum, doc_count, _ = lax.associative_scan(merge_docs, (scores, unit_counts, flags))
    return (scores, doc_sum / jnp.sqrt(doc_count)[:, None])
```

```python
import functools
import jax
import jax.numpy as jnp
from jax import lax
from jax.experimental import pallas as pl
from jax.experimental.pallas import tpu as pltpu
from jax.sharding import PartitionSpec as P

RANK = 32
LANES = 128
F32 = jnp.float32


def swap(value, axis, offset):
    size = lax.axis_size(axis)
    return lax.ppermute(value, axis, [(i, i ^ offset) for i in range(size)])


def stage_bits(size):
    bits = []
    bit = 4
    while bit < size:
        bits.append(bit)
        bit *= 2
    pairs = [bits[i : i + 2] for i in range(0, len(bits), 2)]
    stages = []
    for pair in pairs:
        offsets = [0]
        for one in pair:
            offsets = offsets + [one | other for other in offsets]
        stages.append(offsets)
    return stages


def block_order(stages):
    order = [0]
    for offsets in stages:
        order = [high | low for high in offsets for low in order]
    return order


def project_kernel(halves, with_add, ids, left, right, acts, grads, *rest):
    outs = rest[1:] if with_add else rest
    a = jnp.dot(left[...], acts[...], preferred_element_type=F32)
    b = jnp.dot(right[...], grads[...], preferred_element_type=F32)
    rows = a.shape[0] // halves
    pieces = []
    for h in range(halves):
        pieces.append(a[h * rows : (h + 1) * rows])
        pieces.append(b[h * rows : (h + 1) * rows])
    for h, piece in enumerate(pieces):
        if with_add:
            piece = piece + rest[0][0, h * rows : (h + 1) * rows, :]
        if len(outs) == 1:
            outs[0][0, h * rows : (h + 1) * rows, :] = piece
        else:
            outs[h // 2][0, (h % 2) * rows : (h % 2 + 1) * rows, :] = piece


def project(ids, left, right, acts, grads, halves, add=None, skip=0, split=False):
    blocks = ids.shape[0]
    rows, left_depth = left.shape
    right_depth = right.shape[1]
    total = 2 * rows
    in_specs = [
        pl.BlockSpec((rows, left_depth), lambda i, ids: (0, 0)),
        pl.BlockSpec((rows, right_depth), lambda i, ids: (0, 0)),
        pl.BlockSpec((left_depth, LANES), lambda i, ids: (0, ids[i])),
        pl.BlockSpec((right_depth, LANES), lambda i, ids: (0, ids[i])),
    ]
    args = [left, right, acts, grads]
    if add is not None:
        in_specs.append(pl.BlockSpec((1, total, LANES), lambda i, ids: (i + skip, 0, 0)))
        args.append(add)
    parts = halves if split else 1
    shape = jax.ShapeDtypeStruct((blocks, total // parts, LANES), F32)
    spec = pl.BlockSpec((1, total // parts, LANES), lambda i, ids: (i, 0, 0))
    return pl.pallas_call(
        functools.partial(project_kernel, halves, add is not None),
        grid_spec=pltpu.PrefetchScalarGridSpec(
            num_scalar_prefetch=1,
            grid=(blocks,),
            in_specs=in_specs,
            out_specs=[spec] * parts,
        ),
        out_shape=[shape] * parts,
        cost_estimate=pl.CostEstimate(
            flops=2 * blocks * LANES * rows * (left_depth + right_depth),
            bytes_accessed=2 * blocks * LANES * (left_depth + right_depth)
            + 4 * blocks * total * LANES,
            transcendentals=0,
        ),
        name="project",
    )(ids, *args)


def merge_kernel(count, *refs):
    ins, outs = refs[:count], refs[count:]
    size = outs[0].shape[0]
    for p, out in enumerate(outs):
        value = ins[0][p * size : (p + 1) * size]
        for other in ins[1:]:
            value = value + other[p * size : (p + 1) * size]
        out[...] = value


def merge(parts, pieces):
    blocks, rows, lanes = parts[0].shape
    shape = jax.ShapeDtypeStruct((blocks // pieces, rows, lanes), F32)
    nbytes = 4 * blocks * rows * lanes * (len(parts) + 1)
    return pl.pallas_call(
        functools.partial(merge_kernel, len(parts)),
        out_shape=[shape] * pieces,
        cost_estimate=pl.CostEstimate(
            flops=nbytes // 4, bytes_accessed=nbytes, transcendentals=0
        ),
        name="merge",
    )(*parts)


def score_kernel(count, queries, *refs):
    ins, out = refs[:count], refs[count]
    value = ins[0][0]
    for other in ins[1:]:
        value = value + other[0]
    half = value.shape[0] // 2
    product = value[:half] * value[half:]
    out[...] = product.reshape(queries, half // queries, LANES).sum(axis=1)


def partial_scores(parts, queries):
    return pl.pallas_call(
        functools.partial(score_kernel, len(parts), queries),
        out_shape=jax.ShapeDtypeStruct((queries, LANES), F32),
        name="partial_scores",
    )(*parts)


def tail_kernel(count, *refs):
    ins = refs[:count]
    weights, same_doc, counts, flag, scores, local, message = refs[count:]
    half = count // 2
    rows = [ins[i][...] + ins[i + half][...] for i in range(half)]
    value = jnp.concatenate(rows, axis=0) * weights[...]
    scores[...] = value
    total = jnp.dot(
        value, same_doc[...], precision=lax.Precision.HIGHEST, preferred_element_type=F32
    )
    local[...] = total
    queries = total.shape[0]
    message[0:queries, :] = total
    message[queries : queries + 1, :] = counts[...]
    message[queries + 1 : queries + 2, :] = flag[...]
    message[queries + 2 :, :] = jnp.zeros_like(message[queries + 2 :, :])


def fold_members(queries, me, refs, shift):
    members = len(refs)
    lane = LANES - 1
    tails = [ref[:, lane : lane + 1] for ref in refs]
    mine = lax.rem(lax.shift_right_logical(me, shift), members)
    before = jnp.zeros_like(tails[0])
    running = jnp.zeros_like(tails[0])
    flag_row = lax.broadcasted_iota(jnp.int32, tails[0].shape, 0) == queries + 1
    for j in range(members):
        before = jnp.where(mine == j, running, before)
        value = tails[0]
        for k in range(1, members):
            value = jnp.where((mine ^ k) == j, tails[k], value)
        flag = value[queries + 1 : queries + 2, :]
        kept = jnp.where(flag > 0, value, value + running)
        running = jnp.where(flag_row, jnp.maximum(value, running), kept)
    return before, running


def group_kernel(queries, shift, count, me, *refs):
    before, running = fold_members(queries, me[0], refs[:count], shift)
    refs[count][...] = jnp.broadcast_to(before, refs[count].shape)
    refs[count + 1][...] = jnp.broadcast_to(running, refs[count + 1].shape)


def fold_group(me, messages, queries, shift):
    shape = jax.ShapeDtypeStruct(messages[0].shape, F32)
    return pl.pallas_call(
        functools.partial(group_kernel, queries, shift, len(messages)),
        in_specs=[pl.BlockSpec(memory_space=pltpu.SMEM)]
        + [pl.BlockSpec(memory_space=pltpu.VMEM)] * len(messages),
        out_shape=[shape] * 2,
        name="fold_group",
    )(me, *messages)


def finish_kernel(queries, count, *refs):
    befores = refs[:count]
    local, counts, leading, out = refs[count:]
    carry = jnp.zeros_like(befores[0][...])
    for ref in befores:
        value = ref[...]
        flag = value[queries + 1 : queries + 2, :]
        carry = jnp.where(flag > 0, value, value + carry)
    lead = leading[...]
    total = local[...] + lead * carry[0:queries, :]
    number = counts[...] + lead * carry[queries : queries + 1, :]
    out[...] = total / jnp.sqrt(number)


def local(
    activations, out_grads, left_factors, right_factors, token_ids, doc_starts, token_weights
):
    size, groups = lax.axis_size("loop"), lax.axis_size("groups")
    me = lax.axis_index("loop").astype(jnp.int32)
    rows = left_factors.shape[0]
    queries = rows * size // RANK
    part = rows // groups
    group = lax.axis_index("groups")
    depths = (left_factors.shape[1] // size, right_factors.shape[1] // size)

    def cut(factors, depth):
        mine = lax.dynamic_slice_in_dim(factors, group * part, part, axis=0)
        return mine.reshape(part, size, depth).swapaxes(0, 1)

    outgoing = jnp.concatenate(
        [cut(left_factors, depths[0]), cut(right_factors, depths[1])], axis=2
    )
    arrived = lax.all_to_all(outgoing, "loop", split_axis=0, concat_axis=0, tiled=True)
    own = arrived.reshape(size * part, sum(depths))
    other = lax.ppermute(own, "groups", [(i, i ^ 1) for i in range(groups)])

    stages = stage_bits(size)
    order = jnp.array(block_order(stages), jnp.int32)
    count = len(block_order(stages))
    ids_core = jnp.concatenate([order ^ 2 ^ 1, order ^ 1]) ^ me
    ids_y = (order ^ 2) ^ me
    ids_own = order ^ me

    halves = 2
    partials = []
    for factors in (own, other):
        left, right = factors[:, : depths[0]], factors[:, depths[0] :]
        (send,) = project(ids_core, left, right, activations, out_grads, halves)
        from_core = swap(send, "loop", 1)
        to_y = project(
            ids_y, left, right, activations, out_grads, halves, add=from_core, split=True
        )
        kept = project(
            ids_own,
            left,
            right,
            activations,
            out_grads,
            halves,
            add=from_core,
            skip=count,
            split=True,
        )
        for h in range(halves):
            values = [kept[h], swap(to_y[h], "loop", 2)]
            for offsets in reversed(stages):
                pieces = merge(values, len(offsets))
                values = [pieces[0]] + [
                    swap(piece, "loop", offset) for piece, offset in zip(pieces[1:], offsets[1:])
                ]
            partials.append(partial_scores(values, queries // halves))

    positions = jnp.arange(LANES)
    segment = jnp.cumsum(doc_starts)
    same_doc = (
        (positions[:, None] <= positions[None, :]) & (segment[:, None] == segment[None, :])
    ).astype(F32)
    local_count = jnp.sum(same_doc, axis=0)[None, :]
    leading = (segment == 0).astype(F32)[None, :]
    flag = jnp.broadcast_to((segment[-1] > 0).astype(F32), (1, LANES))
    weights = (jnp.take(token_weights, token_ids) * RANK ** (-0.5))[None, :]

    tile = jax.ShapeDtypeStruct((queries, LANES), F32)
    scores, local_sum, message = pl.pallas_call(
        functools.partial(tail_kernel, len(partials)),
        out_shape=[tile, tile, jax.ShapeDtypeStruct((2 * queries, LANES), F32)],
        name="tails",
    )(*partials, weights, same_doc, local_count, flag)

    befores = []
    shift = 0
    for offsets in [[0, 1, 2, 3]] + stages:
        messages = [message] + [swap(message, "loop", offset) for offset in offsets[1:]]
        before, message = fold_group(me.reshape(1), messages, queries, shift)
        befores.insert(0, before)
        shift += len(offsets).bit_length() - 1
    influence = pl.pallas_call(
        functools.partial(finish_kernel, queries, len(befores)),
        out_shape=tile,
        name="finish",
    )(*befores, local_sum, local_count, leading)
    return (scores.T, influence.T)


def solution(mesh):
    return jax.shard_map(
        local,
        mesh=mesh,
        in_specs=(
            P("loop", "groups"),
            P("loop", "groups"),
            P("loop", None),
            P("loop", None),
            P(("groups", "loop")),
            P(("groups", "loop")),
            P(),
        ),
        out_specs=(P(("groups", "loop"), None), P(("groups", "loop"), None)),
        check_vma=False,
    )
```

```python
import functools
import math
import jax
import jax.numpy as jnp
from jax import lax
from jax.experimental import pallas as pl
from jax.experimental.pallas import tpu as pltpu
from jax.sharding import PartitionSpec as P

RANK = 32
LANES = 128
HALVES = 4
WIDTH = [4, 4, 4, 4]
PIECES = 4
F32 = jnp.float32


def swap(value, axis, offset):
    size = lax.axis_size(axis)
    return lax.ppermute(value, axis, [(i, i ^ offset) for i in range(size)])


def later_stages(size):
    stages = []
    bit = 4
    while bit < size:
        width = min(4, size // bit)
        stages.append([bit * k for k in range(width)])
        bit *= width
    return stages


def place(index, count):
    offset = 0
    bit = 1
    while bit < count:
        offset = offset * 2 + (index // bit) % 2
        bit *= 2
    return 4 * offset


def room(*arrays):
    total = sum(math.prod(a.shape) * jnp.dtype(a.dtype).itemsize for a in arrays)
    return pltpu.CompilerParams(vmem_limit_bytes=total + (4 << 20))


def arrange_kernel(me, acts, grads, *rest):
    outs, sems = rest[:-1], rest[-1]
    depth = grads.shape[0]
    per = outs[0].shape[0]
    half = per * len(outs) // 2

    def copies(piece, i):
        block = piece * per + i
        other_core = 1 - block // half
        near = (block % half) // (half // 2)
        offset = place(block % (half // 2), half // 2) + 2 * (1 - near) + other_core
        start = pl.multiple_of((me[0] ^ offset) * LANES, LANES)
        return [
            pltpu.make_async_copy(
                ref.at[:, pl.ds(start, LANES)],
                outs[piece].at[i, pl.ds(row, ref.shape[0])],
                sems.at[k, block],
            )
            for k, (ref, row) in enumerate(((grads, 0), (acts, depth)))
        ]

    def begin(piece, i, _):
        for copy in copies(piece, i):
            copy.start()
        return 0

    def end(piece, i, _):
        for copy in copies(piece, i):
            copy.wait()
        return 0

    for step in (begin, end):
        for piece in range(len(outs)):
            lax.fori_loop(0, per, functools.partial(step, piece), 0)


def arrange(me, acts, grads):
    blocks = acts.shape[1] // LANES
    shape = (blocks // PIECES, grads.shape[0] + acts.shape[0], LANES)
    return pl.pallas_call(
        arrange_kernel,
        in_specs=[pl.BlockSpec(memory_space=pltpu.SMEM)]
        + [pl.BlockSpec(memory_space=pltpu.HBM)] * 2,
        out_shape=[pltpu.VMEM(shape, acts.dtype)] * PIECES,
        scratch_shapes=[pltpu.SemaphoreType.DMA((2, blocks))],
        compiler_params=pltpu.CompilerParams(vmem_limit_bytes=50 << 20),
        cost_estimate=pl.CostEstimate(
            flops=0, bytes_accessed=4 * (acts.size + grads.size), transcendentals=0
        ),
        name="arrange",
    )(me, acts, grads)


def project_kernel(depths, count, factors, *rest):
    columns, outs = rest[:count], rest[count:]
    blocks = outs[0].shape[0]
    per = columns[0].shape[0]
    halves = len(outs)
    size = factors.shape[0] // halves
    gap, right_depth, left_depth = depths

    def pair(ref, base, i, _):
        left = factors[:, gap : gap + left_depth]
        right = factors[:, 0:right_depth]
        two = range(2)
        acts = jnp.concatenate([ref[2 * i + j, right_depth:] for j in two], axis=1)
        grads = jnp.concatenate([ref[2 * i + j, :right_depth] for j in two], axis=1)
        a = jnp.dot(left, acts, preferred_element_type=F32)
        b = jnp.dot(right, grads, preferred_element_type=F32)
        for h, out in enumerate(outs):
            for side, value in enumerate((a, b)):
                piece = value[h * size : (h + 1) * size]
                for j in two:
                    out[base + 2 * i + j, side * size : (side + 1) * size, :] = piece[
                        :, j * LANES : (j + 1) * LANES
                    ]
        return 0

    for k, ref in enumerate(columns):
        step = functools.partial(pair, ref, k * per)
        lax.fori_loop(0, per // 2, step, 0, unroll=blocks <= 8)


def project(factors, depths, columns, halves):
    blocks = columns[0].shape[0] * len(columns)
    rows = factors.shape[0]
    shape = jax.ShapeDtypeStruct((blocks, 2 * rows // halves, LANES), F32)
    size = sum(c.size for c in columns)
    return pl.pallas_call(
        functools.partial(project_kernel, depths, len(columns)),
        out_shape=[shape] * halves,
        compiler_params=room(factors, *columns, *[shape] * halves),
        cost_estimate=pl.CostEstimate(
            flops=2 * size * rows, bytes_accessed=2 * size, transcendentals=0
        ),
        name="project",
    )(factors, *columns)


def merge_kernel(starts, *refs):
    ins, outs = refs[: len(starts)], refs[len(starts) :]
    size = outs[0].shape[0]
    for p, out in enumerate(outs):
        value = ins[0][starts[0] + p * size : starts[0] + (p + 1) * size]
        for start, other in zip(starts[1:], ins[1:]):
            value = value + other[start + p * size : start + (p + 1) * size]
        out[...] = value


def merge(parts, starts, blocks, pieces):
    shape = jax.ShapeDtypeStruct((blocks // pieces,) + parts[0].shape[1:], F32)
    nbytes = 4 * math.prod(shape.shape) * pieces * (len(parts) + 1)
    return pl.pallas_call(
        functools.partial(merge_kernel, starts),
        out_shape=[shape] * pieces,
        compiler_params=room(*parts, *[shape] * pieces),
        cost_estimate=pl.CostEstimate(
            flops=nbytes // 4, bytes_accessed=nbytes, transcendentals=0
        ),
        name="merge",
    )(*parts)


def rank_sums(refs, queries):
    value = refs[0][0]
    for other in refs[1:]:
        value = value + other[0]
    half = value.shape[0] // 2
    product = value[:half] * value[half:]
    return product.reshape(queries, half // queries, LANES).sum(axis=1)


def partial_kernel(queries, *refs):
    refs[-1][...] = rank_sums(refs[:-1], queries)


def partial_scores(parts, queries):
    return pl.pallas_call(
        functools.partial(partial_kernel, queries),
        out_shape=jax.ShapeDtypeStruct((queries, LANES), F32),
        compiler_params=room(*parts),
        name="partial_scores",
    )(*parts)


def tail_kernel(count, halves, queries, *refs):
    ready, last = refs[:count], refs[count:-4]
    weights, doc_starts, scores, message = refs[-4:]
    parts = [ref[...] for ref in ready] + [rank_sums(last, queries // halves)]
    rows = []
    for h in range(halves):
        rows.append(functools.reduce(jnp.add, parts[h::halves]))
    value = jnp.concatenate(rows, axis=0) * weights[...]
    scores[...] = value
    lane = lax.broadcasted_iota(jnp.int32, (8, LANES), 1)
    start = jnp.where(doc_starts[...] > 0, lane, -1)
    step = 1
    while step < LANES:
        start = jnp.maximum(start, jnp.where(lane >= step, pltpu.roll(start, step, 1), -1))
        step *= 2
    start = start[0:1, :]
    lane = lane[0:1, :]
    earlier = lax.broadcasted_iota(jnp.int32, (LANES, LANES), 0)
    same_doc = ((earlier >= start) & (earlier <= lane)).astype(F32)
    total = jnp.dot(
        value, same_doc, precision=lax.Precision.HIGHEST, preferred_element_type=F32
    )
    number = (lane - jnp.maximum(start, 0) + 1).astype(F32)
    started = (start >= 0).astype(F32)
    message[0:queries, :] = total
    message[queries : queries + 1, :] = number
    message[queries + 1 : queries + 2, :] = started
    message[queries + 2 : queries + 3, :] = 1.0 - started
    message[queries + 3 :, :] = jnp.zeros_like(message[queries + 3 :, :])


def fold_members(queries, me, refs, shift):
    members = len(refs)
    tails = [ref[:, LANES - 1 : LANES] for ref in refs]
    mine = lax.rem(lax.shift_right_logical(me, shift), members)
    before = jnp.zeros_like(tails[0])
    running = jnp.zeros_like(tails[0])
    flag_row = lax.broadcasted_iota(jnp.int32, tails[0].shape, 0) == queries + 1
    for j in range(members):
        before = jnp.where(mine == j, running, before)
        value = tails[0]
        for k in range(1, members):
            value = jnp.where((mine ^ k) == j, tails[k], value)
        flag = value[queries + 1 : queries + 2, :]
        kept = jnp.where(flag > 0, value, value + running)
        running = jnp.where(flag_row, jnp.maximum(value, running), kept)
    return before, running


def group_kernel(queries, shift, me, *refs):
    before, running = fold_members(queries, me[0], refs[:-2], shift)
    refs[-2][...] = jnp.broadcast_to(before, refs[-2].shape)
    refs[-1][...] = jnp.broadcast_to(running, refs[-1].shape)


def fold_group(me, messages, queries, shift):
    shape = jax.ShapeDtypeStruct(messages[0].shape, F32)
    return pl.pallas_call(
        functools.partial(group_kernel, queries, shift),
        in_specs=[pl.BlockSpec(memory_space=pltpu.SMEM)]
        + [pl.BlockSpec(memory_space=pltpu.VMEM)] * len(messages),
        out_shape=[shape] * 2,
        compiler_params=room(),
        name="fold_group",
    )(me, *messages)


def finish_kernel(queries, shift, members, me, *refs):
    own, out = refs[-2:]
    before, _ = fold_members(queries, me[0], refs[:members], shift)
    carry = before
    for ref in refs[members:-2]:
        value = ref[:, LANES - 1 : LANES]
        flag = value[queries + 1 : queries + 2, :]
        carry = jnp.where(flag > 0, value, value + carry)
    lead = own[queries + 2 : queries + 3, :]
    total = own[0:queries, :] + lead * carry[0:queries, :]
    number = own[queries : queries + 1, :] + lead * carry[queries : queries + 1, :]
    out[...] = total / jnp.sqrt(number)


def local(
    activations, out_grads, left_factors, right_factors, token_ids, doc_starts, token_weights
):
    size = lax.axis_size("loop")
    me = lax.axis_index("loop").astype(jnp.int32).reshape(1)
    rows = left_factors.shape[0]
    queries = rows * size // RANK
    part = rows
    depths = (left_factors.shape[1] // size, right_factors.shape[1] // size)

    def cut(factors, depth):
        return factors.reshape(part, size, depth).swapaxes(0, 1)

    depth = -(-depths[1] // LANES) * LANES
    gap = jnp.zeros((size, part, depth - depths[1]), left_factors.dtype)
    outgoing = jnp.concatenate(
        [cut(right_factors, depths[1]), gap, cut(left_factors, depths[0])], axis=2
    )
    arrived = lax.all_to_all(outgoing, "loop", split_axis=0, concat_axis=0, tiled=True)
    columns = arrange(me, activations, out_grads)
    arrived, columns = lax.optimization_barrier((arrived, columns))
    own = arrived.reshape(size * part, depth + depths[0])
    stages = later_stages(size)
    count = size // 4
    halves = HALVES
    bounds = (depth, depths[1], depths[0])
    bounds = (depth, depths[1], depths[0])
    sent = project(own, bounds, columns[: PIECES // 2], halves)
    from_core = [swap(part, "loop", 1) for part in sent]
    kept = project(own, bounds, columns[PIECES // 2 :], halves)
    to_y = [merge([kept[h], from_core[h]], [0, 0], count, 1)[0] for h in range(halves)]
    from_y = [swap(part, "loop", 2) for part in to_y]
    ready = []
    wave = []
    for h in range(halves):
        if len(ready) > 1:
            from_y[h], ready[-2] = lax.optimization_barrier((from_y[h], ready[-2]))
        if wave:
            from_y[h], *wave = lax.optimization_barrier((from_y[h], *wave))
        values = [kept[h], from_core[h], from_y[h]]
        starts = [count, count, 0]
        blocks = count
        bit = 4
        wave = []
        while bit < size:
            width = WIDTH[h] if 2 * bit < size else 2
            pieces = merge(values, starts, blocks, width)
            if width == 2:
                values = [pieces[0], swap(pieces[1], "loop", bit)]
                wave = [pieces[1]]
            else:
                values = [pieces[0]] + [
                    swap(pieces[k], "loop", offset)
                    for k, offset in ((1, 2 * bit), (2, bit), (3, 3 * bit))
                ]
            blocks //= width
            starts = [0] * width
            bit *= width
        ready.append(partial_scores(values, queries // halves) if h + 1 < halves else values)
    last = ready.pop()

    weights = jnp.take(token_weights, token_ids, mode="clip") * RANK ** (-0.5)
    tile = jax.ShapeDtypeStruct((queries, LANES), F32)
    scores, message = pl.pallas_call(
        functools.partial(tail_kernel, len(ready), halves, queries),
        out_shape=[tile, jax.ShapeDtypeStruct((2 * queries, LANES), F32)],
        compiler_params=room(),
        name="tails",
    )(*ready, *last, weights[None, :], doc_starts[None, :])

    own_message = message
    befores = []
    shift = 0
    rounds = [[0, 1, 2, 3]] + stages
    for offsets in rounds[:-1]:
        messages = [message] + [swap(message, "loop", offset) for offset in offsets[1:]]
        before, message = fold_group(me, messages, queries, shift)
        befores.insert(0, before)
        shift += len(offsets).bit_length() - 1
    messages = [message] + [swap(message, "loop", offset) for offset in rounds[-1][1:]]
    influence = pl.pallas_call(
        functools.partial(finish_kernel, queries, shift, len(messages)),
        in_specs=[pl.BlockSpec(memory_space=pltpu.SMEM)]
        + [pl.BlockSpec(memory_space=pltpu.VMEM)] * (len(messages) + len(befores) + 1),
        out_shape=tile,
        compiler_params=room(),
        name="finish",
    )(me, *messages, *befores, own_message)
    return (scores.T, influence.T)


def solution(mesh):
    return jax.shard_map(
        local,
        mesh=mesh,
        in_specs=(
            P("loop", "groups"),
            P("loop", "groups"),
            P("loop", None),
            P("loop", None),
            P(("groups", "loop")),
            P(("groups", "loop")),
            P(),
        ),
        out_specs=(P(("groups", "loop"), None), P(("groups", "loop"), None)),
        check_vma=False,
    )
```

```python
import functools
import math
import jax
import jax.numpy as jnp
from jax import lax
from jax.experimental import pallas as pl
from jax.experimental.pallas import tpu as pltpu
from jax.sharding import PartitionSpec as P

RANK = 32
LANES = 128
PIECES = 4
CHUNKS = ((1,), (1,))
F32 = jnp.float32


def swap(value, axis, offset):
    size = lax.axis_size(axis)
    return lax.ppermute(value, axis, [(i, i ^ offset) for i in range(size)])


def later_stages(size):
    stages = []
    bit = 4
    while bit < size:
        width = min(4, size // bit)
        stages.append([bit * k for k in range(width)])
        bit *= width
    return stages


def place(index, count):
    offset = 0
    bit = 1
    while bit < count:
        offset = offset * 2 + (index // bit) % 2
        bit *= 2
    return 4 * offset


def room(*arrays):
    total = sum(math.prod(a.shape) * jnp.dtype(a.dtype).itemsize for a in arrays)
    return pltpu.CompilerParams(vmem_limit_bytes=total + (4 << 20))


def arrange_kernel(me, acts, grads, *rest):
    outs, sems = rest[:-1], rest[-1]
    depth = grads.shape[0]
    per = outs[0].shape[0]
    half = per * len(outs) // 2

    def copies(piece, i):
        block = piece * per + i
        other_core = 1 - block // half
        near = (block % half) // (half // 2)
        offset = place(block % (half // 2), half // 2) + 2 * (1 - near) + other_core
        start = pl.multiple_of((me[0] ^ offset) * LANES, LANES)
        return [
            pltpu.make_async_copy(
                ref.at[:, pl.ds(start, LANES)],
                outs[piece].at[i, pl.ds(row, ref.shape[0])],
                sems.at[k, block],
            )
            for k, (ref, row) in enumerate(((grads, 0), (acts, depth)))
        ]

    def begin(piece, i, _):
        for copy in copies(piece, i):
            copy.start()
        return 0

    def end(piece, i, _):
        for copy in copies(piece, i):
            copy.wait()
        return 0

    for step in (begin, end):
        for piece in range(len(outs)):
            lax.fori_loop(0, per, functools.partial(step, piece), 0)


def arrange(me, acts, grads):
    blocks = acts.shape[1] // LANES
    shape = (blocks // PIECES, grads.shape[0] + acts.shape[0], LANES)
    return pl.pallas_call(
        arrange_kernel,
        in_specs=[pl.BlockSpec(memory_space=pltpu.SMEM)]
        + [pl.BlockSpec(memory_space=pltpu.HBM)] * 2,
        out_shape=[pltpu.VMEM(shape, acts.dtype)] * PIECES,
        scratch_shapes=[pltpu.SemaphoreType.DMA((2, blocks))],
        compiler_params=pltpu.CompilerParams(vmem_limit_bytes=50 << 20),
        cost_estimate=pl.CostEstimate(
            flops=0, bytes_accessed=4 * (acts.size + grads.size), transcendentals=0
        ),
        name="arrange",
    )(me, acts, grads)


def project_kernel(depths, count, factors, *rest):
    columns, outs = rest[:count], rest[count:]
    blocks = outs[0].shape[0]
    per = columns[0].shape[0]
    gap, right_depth, left_depth = depths

    def pair(ref, base, i, _):
        left = factors[:, gap : gap + left_depth]
        right = factors[:, 0:right_depth]
        two = range(2)
        acts = jnp.concatenate([ref[2 * i + j, right_depth:] for j in two], axis=1)
        grads = jnp.concatenate([ref[2 * i + j, :right_depth] for j in two], axis=1)
        a = jnp.dot(left, acts, preferred_element_type=F32)
        b = jnp.dot(right, grads, preferred_element_type=F32)
        first = 0
        for out in outs:
            size = out.shape[1] // 2
            for side, value in enumerate((a, b)):
                piece = value[first : first + size]
                for j in two:
                    out[base + 2 * i + j, side * size : (side + 1) * size, :] = piece[
                        :, j * LANES : (j + 1) * LANES
                    ]
            first += size
        return 0

    for k, ref in enumerate(columns):
        step = functools.partial(pair, ref, k * per)
        lax.fori_loop(0, per // 2, step, 0, unroll=blocks <= 8)


def project(factors, depths, columns, waves):
    blocks = columns[0].shape[0] * len(columns)
    shapes = [jax.ShapeDtypeStruct((blocks, 2 * w, LANES), F32) for w in waves]
    size = sum(c.size for c in columns)
    return pl.pallas_call(
        functools.partial(project_kernel, depths, len(columns)),
        out_shape=shapes,
        compiler_params=room(factors, *columns, *shapes),
        cost_estimate=pl.CostEstimate(
            flops=2 * size * factors.shape[0], bytes_accessed=2 * size, transcendentals=0
        ),
        name="project",
    )(factors, *columns)


def message_rows(blocks, rows):
    return blocks * rows // 4 * 3 + -(-blocks // 8) * 8


def encode(out, block, blocks, value):
    size = value.shape[0] // 4
    codes, powers = [], None
    for g in range(4):
        group = value[g * size : (g + 1) * size]
        most = jnp.max(jnp.abs(group), axis=0, keepdims=True)
        power = jnp.clip(jnp.floor(jnp.log(most) * (1 / math.log(2.0))) + 2.0, -100.0, 100.0)
        codes.append(jnp.floor(group * jnp.exp2(23.0 - power) + 0.5).astype(jnp.int32))
        byte = (power.astype(jnp.int32) + 128) << (8 * g)
        powers = byte if powers is None else powers | byte
    for g in range(3):
        high = lax.shift_right_arithmetic(codes[3], 8 * g) << 24
        words = (codes[g] & 0xFFFFFF) | high
        out[pl.ds((3 * block + g) * size, size), :] = words
    out[pl.ds(3 * blocks * size + block, 1), :] = powers


def decode(ref, block, blocks, rows):
    size = rows // 4
    words = [ref[pl.ds((3 * block + g) * size, size), :] for g in range(3)]
    powers = ref[pl.ds(3 * blocks * size + block, 1), :]
    codes = [lax.shift_right_arithmetic(word << 8, 8) for word in words]
    low = lax.shift_right_logical(words[0], 24) | (lax.shift_right_logical(words[1], 24) << 8)
    codes.append(low | (lax.shift_right_arithmetic(words[2], 24) << 16))
    groups = []
    for g, code in enumerate(codes):
        power = (lax.shift_right_logical(powers, 8 * g) & 0xFF) - 128
        groups.append(code.astype(F32) * jnp.exp2(power.astype(F32) - 23.0))
    return jnp.concatenate(groups, axis=0)


def total_of(refs, starts, block, blocks, rows):
    value = None
    for ref, start in zip(refs, starts):
        term = decode(ref, block, blocks, rows) if start is None else ref[start + block]
        value = term if value is None else value + term
    return value


def merge_kernel(starts, blocks, rows, stay, *refs):
    ins, outs = refs[: len(starts)], refs[len(starts) :]
    size = blocks // len(outs)
    for p, out in enumerate(outs):

        def step(i, _):
            value = total_of(ins, starts, p * size + i, blocks, rows)
            if stay and p == 0:
                out[i] = value
            else:
                encode(out, i, size, value)
            return 0

        lax.fori_loop(0, size, step, 0, unroll=blocks <= 8)


def merge(parts, starts, blocks, pieces, stay=True):
    rows = parts[0].shape[1]
    size = blocks // pieces
    message = jax.ShapeDtypeStruct((message_rows(size, rows), LANES), jnp.int32)
    first = jax.ShapeDtypeStruct((size, rows, LANES), F32)
    shapes = [first if stay else message] + [message] * (pieces - 1)
    nbytes = 4 * blocks * rows * LANES * (len(parts) + 1)
    return pl.pallas_call(
        functools.partial(merge_kernel, starts, blocks, rows, stay),
        out_shape=shapes,
        compiler_params=room(*parts, *shapes),
        cost_estimate=pl.CostEstimate(
            flops=nbytes // 4, bytes_accessed=nbytes, transcendentals=0
        ),
        name="merge",
    )(*parts)


def rank_sums(refs, ranks):
    rows = refs[0].shape[1]
    starts = [0] + [None] * (len(refs) - 1)
    value = total_of(refs, starts, 0, 1, rows)
    product = value[: rows // 2] * value[rows // 2 :]
    return product.reshape(rows // 2 // ranks, ranks, LANES).sum(axis=1)


def partial_kernel(ranks, *refs):
    refs[-1][...] = rank_sums(refs[:-1], ranks)


def partial_scores(parts, ranks):
    queries = parts[0].shape[1] // 2 // ranks
    return pl.pallas_call(
        functools.partial(partial_kernel, ranks),
        out_shape=jax.ShapeDtypeStruct((queries, LANES), F32),
        compiler_params=room(*parts),
        name="partial_scores",
    )(*parts)


def tail_kernel(count, queries, ranks, *refs):
    ready, last = refs[:count], refs[count:-4]
    weights, doc_starts, scores, message = refs[-4:]
    parts = [ref[...] for ref in ready] + [rank_sums(last, ranks)]
    value = None
    while parts:
        chunk = []
        while sum(part.shape[0] for part in chunk) < queries:
            chunk.append(parts.pop(0))
        chunk = jnp.concatenate(chunk, axis=0)
        value = chunk if value is None else value + chunk
    value = value * weights[...]
    scores[...] = value
    lane = lax.broadcasted_iota(jnp.int32, (8, LANES), 1)
    start = jnp.where(doc_starts[...] > 0, lane, -1)
    step = 1
    while step < LANES:
        start = jnp.maximum(start, jnp.where(lane >= step, pltpu.roll(start, step, 1), -1))
        step *= 2
    start = start[0:1, :]
    lane = lane[0:1, :]
    earlier = lax.broadcasted_iota(jnp.int32, (LANES, LANES), 0)
    same_doc = ((earlier >= start) & (earlier <= lane)).astype(F32)
    total = jnp.dot(
        value, same_doc, precision=lax.Precision.HIGHEST, preferred_element_type=F32
    )
    number = (lane - jnp.maximum(start, 0) + 1).astype(F32)
    started = (start >= 0).astype(F32)
    message[0:queries, :] = total
    message[queries : queries + 1, :] = number
    message[queries + 1 : queries + 2, :] = started
    message[queries + 2 : queries + 3, :] = 1.0 - started
    message[queries + 3 :, :] = jnp.zeros_like(message[queries + 3 :, :])


def fold_members(queries, me, refs, shift):
    members = len(refs)
    tails = [ref[:, LANES - 1 : LANES] for ref in refs]
    mine = lax.rem(lax.shift_right_logical(me, shift), members)
    before = jnp.zeros_like(tails[0])
    running = jnp.zeros_like(tails[0])
    flag_row = lax.broadcasted_iota(jnp.int32, tails[0].shape, 0) == queries + 1
    for j in range(members):
        before = jnp.where(mine == j, running, before)
        value = tails[0]
        for k in range(1, members):
            value = jnp.where((mine ^ k) == j, tails[k], value)
        flag = value[queries + 1 : queries + 2, :]
        kept = jnp.where(flag > 0, value, value + running)
        running = jnp.where(flag_row, jnp.maximum(value, running), kept)
    return before, running


def group_kernel(queries, shift, me, *refs):
    before, running = fold_members(queries, me[0], refs[:-2], shift)
    refs[-2][...] = jnp.broadcast_to(before, refs[-2].shape)
    refs[-1][...] = jnp.broadcast_to(running, refs[-1].shape)


def fold_group(me, messages, queries, shift):
    shape = jax.ShapeDtypeStruct(messages[0].shape, F32)
    return pl.pallas_call(
        functools.partial(group_kernel, queries, shift),
        in_specs=[pl.BlockSpec(memory_space=pltpu.SMEM)]
        + [pl.BlockSpec(memory_space=pltpu.VMEM)] * len(messages),
        out_shape=[shape] * 2,
        compiler_params=room(),
        name="fold_group",
    )(me, *messages)


def finish_kernel(queries, shift, members, me, *refs):
    own, out = refs[-2:]
    before, _ = fold_members(queries, me[0], refs[:members], shift)
    carry = before
    for ref in refs[members:-2]:
        value = ref[:, LANES - 1 : LANES]
        flag = value[queries + 1 : queries + 2, :]
        carry = jnp.where(flag > 0, value, value + carry)
    lead = own[queries + 2 : queries + 3, :]
    total = own[0:queries, :] + lead * carry[0:queries, :]
    number = own[queries : queries + 1, :] + lead * carry[queries : queries + 1, :]
    out[...] = total / jnp.sqrt(number)


def local(
    activations, out_grads, left_factors, right_factors, token_ids, doc_starts, token_weights
):
    size, groups = lax.axis_size("loop"), lax.axis_size("groups")
    me = lax.axis_index("loop").astype(jnp.int32).reshape(1)
    rows = left_factors.shape[0]
    queries = rows * size // RANK
    part = rows // groups
    group = lax.axis_index("groups")
    depths = (left_factors.shape[1] // size, right_factors.shape[1] // size)

    def cut(factors, depth):
        mine = lax.dynamic_slice_in_dim(factors, group * part, part, axis=0)
        return mine.reshape(part, size, depth).swapaxes(0, 1)

    depth = -(-depths[1] // LANES) * LANES
    gap = jnp.zeros((size, part, depth - depths[1]), left_factors.dtype)
    outgoing = jnp.concatenate(
        [cut(right_factors, depths[1]), gap, cut(left_factors, depths[0])], axis=2
    )
    arrived = lax.all_to_all(outgoing, "loop", split_axis=0, concat_axis=0, tiled=True)
    columns = arrange(me, activations, out_grads)
    weights = jnp.take(token_weights, token_ids, mode="clip") * RANK ** (-0.5)
    arrived, columns, weights = lax.optimization_barrier((arrived, columns, weights))
    own = arrived.reshape(size * part, depth + depths[0])
    stages = later_stages(size)
    count = size // 4
    bounds = (depth, depths[1], depths[0])
    ranks = RANK // groups
    other = lax.ppermute(own, "groups", [(i, i ^ 1) for i in range(groups)])
    flows = []
    for factors, waves in zip((own, other), CHUNKS):
        if flows:
            factors, flows[-1][2] = lax.optimization_barrier((factors, flows[-1][2]))
        waves = [factors.shape[0] // w for w in waves]
        sent = project(factors, bounds, columns[: PIECES // 2], waves)
        from_core = [swap(part, "loop", 1) for part in sent]
        kept = project(factors, bounds, columns[PIECES // 2 :], waves)
        to_y = [merge([k, f], [0, 0], count, 1, stay=False)[0] for k, f in zip(kept, from_core)]
        from_y = [swap(part, "loop", 2) for part in to_y]
        flows.extend([list(flow) for flow in zip(kept, from_core, from_y)])
        if len(flows) > 1:
            flows[0][2], to_y[-1] = lax.optimization_barrier((flows[0][2], to_y[-1]))
    ready = []
    for h, values in enumerate(flows):
        if len(ready) > 1:
            values[2], ready[-2] = lax.optimization_barrier((values[2], ready[-2]))
        starts = [count, count, None]
        blocks = count
        bit = 4
        while bit < size:
            width = 4 if 2 * bit < size else 2
            pieces = merge(values, starts, blocks, width)
            offsets = (0, 2 * bit, bit, 3 * bit) if width == 4 else (0, bit)
            values = [pieces[0]] + [
                swap(piece, "loop", offset) for piece, offset in zip(pieces[1:], offsets[1:])
            ]
            blocks //= width
            starts = [0] + [None] * (width - 1)
            bit *= width
        ready.append(partial_scores(values, ranks) if h + 1 < len(flows) else values)
    last = ready.pop()

    tile = jax.ShapeDtypeStruct((queries, LANES), F32)
    scores, message = pl.pallas_call(
        functools.partial(tail_kernel, len(ready), queries, ranks),
        out_shape=[tile, jax.ShapeDtypeStruct((2 * queries, LANES), F32)],
        compiler_params=room(),
        name="tails",
    )(*ready, *last, weights[None, :], doc_starts[None, :])

    own_message = message
    befores = []
    shift = 0
    rounds = [[0, 1, 2, 3]] + stages
    for offsets in rounds[:-1]:
        messages = [message] + [swap(message, "loop", offset) for offset in offsets[1:]]
        before, message = fold_group(me, messages, queries, shift)
        befores.insert(0, before)
        shift += len(offsets).bit_length() - 1
    messages = [message] + [swap(message, "loop", offset) for offset in rounds[-1][1:]]
    influence = pl.pallas_call(
        functools.partial(finish_kernel, queries, shift, len(messages)),
        in_specs=[pl.BlockSpec(memory_space=pltpu.SMEM)]
        + [pl.BlockSpec(memory_space=pltpu.VMEM)] * (len(messages) + len(befores) + 1),
        out_shape=tile,
        compiler_params=room(),
        name="finish",
    )(me, *messages, *befores, own_message)
    return (scores.T, influence.T)


def solution(mesh):
    return jax.shard_map(
        local,
        mesh=mesh,
        in_specs=(
            P("loop", "groups"),
            P("loop", "groups"),
            P("loop", None),
            P("loop", None),
            P(("groups", "loop")),
            P(("groups", "loop")),
            P(),
        ),
        out_specs=(P(("groups", "loop"), None), P(("groups", "loop"), None)),
        check_vma=False,
    )
```

```python
import functools
import math
import jax
import jax.numpy as jnp
from jax import lax
from jax.experimental import pallas as pl
from jax.experimental.pallas import tpu as pltpu
from jax.sharding import PartitionSpec as P

RANK = 32
LANES = 128
PIECES = 4
CHUNKS = ((1,), (1,))
F32 = jnp.float32
BITS = 18
GROUPS, WORDS = 16, 9
RANGE = 24.0
LEVELS = (1 << (BITS - 1)) - 1


def swap(value, axis, offset):
    size = lax.axis_size(axis)
    return lax.ppermute(value, axis, [(i, i ^ offset) for i in range(size)])


def later_stages(size):
    stages = []
    bit = 4
    while bit < size:
        width = min(4, size // bit)
        stages.append([bit * k for k in range(width)])
        bit *= width
    return stages


def place(index, count):
    offset = 0
    bit = 1
    while bit < count:
        offset = offset * 2 + (index // bit) % 2
        bit *= 2
    return 4 * offset


def room(*arrays):
    total = sum(math.prod(a.shape) * jnp.dtype(a.dtype).itemsize for a in arrays)
    return pltpu.CompilerParams(vmem_limit_bytes=total + (4 << 20))


def arrange_kernel(me, acts, grads, *rest):
    outs, sems = rest[:-1], rest[-1]
    depth = grads.shape[0]
    per = outs[0].shape[0]
    half = per * len(outs) // 2

    def copies(piece, i):
        block = piece * per + i
        other_core = 1 - block // half
        near = (block % half) // (half // 2)
        offset = place(block % (half // 2), half // 2) + 2 * (1 - near) + other_core
        start = pl.multiple_of((me[0] ^ offset) * LANES, LANES)
        return [
            pltpu.make_async_copy(
                ref.at[:, pl.ds(start, LANES)],
                outs[piece].at[i, pl.ds(row, ref.shape[0])],
                sems.at[k, block],
            )
            for k, (ref, row) in enumerate(((grads, 0), (acts, depth)))
        ]

    def begin(piece, i, _):
        for copy in copies(piece, i):
            copy.start()
        return 0

    def end(piece, i, _):
        for copy in copies(piece, i):
            copy.wait()
        return 0

    for step in (begin, end):
        for piece in range(len(outs)):
            lax.fori_loop(0, per, functools.partial(step, piece), 0)


def arrange(me, acts, grads):
    blocks = acts.shape[1] // LANES
    shape = (blocks // PIECES, grads.shape[0] + acts.shape[0], LANES)
    return pl.pallas_call(
        arrange_kernel,
        in_specs=[pl.BlockSpec(memory_space=pltpu.SMEM)]
        + [pl.BlockSpec(memory_space=pltpu.HBM)] * 2,
        out_shape=[pltpu.VMEM(shape, acts.dtype)] * PIECES,
        scratch_shapes=[pltpu.SemaphoreType.DMA((2, blocks))],
        compiler_params=pltpu.CompilerParams(vmem_limit_bytes=50 << 20),
        cost_estimate=pl.CostEstimate(
            flops=0, bytes_accessed=4 * (acts.size + grads.size), transcendentals=0
        ),
        name="arrange",
    )(me, acts, grads)


def project_kernel(depths, count, factors, *rest):
    columns, outs = rest[:count], rest[count:]
    blocks = outs[0].shape[0]
    per = columns[0].shape[0]
    gap, right_depth, left_depth = depths

    def pair(ref, base, i, _):
        left = factors[:, gap : gap + left_depth]
        right = factors[:, 0:right_depth]
        two = range(2)
        acts = jnp.concatenate([ref[2 * i + j, right_depth:] for j in two], axis=1)
        grads = jnp.concatenate([ref[2 * i + j, :right_depth] for j in two], axis=1)
        a = jnp.dot(left, acts, preferred_element_type=F32)
        b = jnp.dot(right, grads, preferred_element_type=F32)
        first = 0
        for out in outs:
            size = out.shape[1] // 2
            for side, value in enumerate((a, b)):
                piece = value[first : first + size]
                for j in two:
                    out[base + 2 * i + j, side * size : (side + 1) * size, :] = piece[
                        :, j * LANES : (j + 1) * LANES
                    ]
            first += size
        return 0

    for k, ref in enumerate(columns):
        step = functools.partial(pair, ref, k * per)
        lax.fori_loop(0, per // 2, step, 0, unroll=blocks <= 8)


def project(factors, depths, columns, waves):
    blocks = columns[0].shape[0] * len(columns)
    shapes = [jax.ShapeDtypeStruct((blocks, 2 * w, LANES), F32) for w in waves]
    size = sum(c.size for c in columns)
    return pl.pallas_call(
        functools.partial(project_kernel, depths, len(columns)),
        out_shape=shapes,
        compiler_params=room(factors, *columns, *shapes),
        cost_estimate=pl.CostEstimate(
            flops=2 * size * factors.shape[0], bytes_accessed=2 * size, transcendentals=0
        ),
        name="project",
    )(factors, *columns)


def message_rows(blocks, rows):
    return blocks * rows // GROUPS * WORDS + -(-blocks // 8) * 8


def spread():
    spare = 32 - BITS
    places = []
    for j in range(GROUPS - WORDS):
        start = j * BITS
        while start < (j + 1) * BITS:
            word = start // spare
            end = min((j + 1) * BITS, (word + 1) * spare)
            places.append((j, word, start - j * BITS, BITS + start - word * spare, end - start))
            start = end
    return places


def encode(out, block, blocks, value):
    size = value.shape[0] // GROUPS
    half = value.shape[0] // 2
    codes, powers = [], None
    for side in range(2):
        part = value[side * half : (side + 1) * half]
        logs = jnp.log(jnp.abs(part)) * (1 / math.log(2.0))
        top = jnp.clip(jnp.ceil(jnp.max(logs, axis=0, keepdims=True)), -100.0, 100.0)
        steps = jnp.maximum((logs + (RANGE - top)) * (LEVELS / RANGE) + 0.5, 0.0)
        code = jnp.minimum(steps, float(LEVELS)).astype(jnp.int32)
        code = jnp.where(part < 0, code | (LEVELS + 1), code)
        codes.extend(code[g * size : (g + 1) * size] for g in range(GROUPS // 2))
        byte = (top.astype(jnp.int32) + 128) << (8 * side)
        powers = byte if powers is None else powers | byte
    words = codes[:WORDS]
    for j, word, low, shift, bits in spread():
        piece = lax.shift_right_logical(codes[WORDS + j], low) & ((1 << bits) - 1)
        words[word] = words[word] | (piece << shift)
    for g, word in enumerate(words):
        out[pl.ds((WORDS * block + g) * size, size), :] = word
    out[pl.ds(WORDS * blocks * size + block, 1), :] = powers


def decode(ref, block, blocks, rows):
    size = rows // GROUPS
    words = [ref[pl.ds((WORDS * block + g) * size, size), :] for g in range(WORDS)]
    powers = ref[pl.ds(WORDS * blocks * size + block, 1), :]
    codes = [word & ((1 << BITS) - 1) for word in words] + [None] * (GROUPS - WORDS)
    for j, word, low, shift, bits in spread():
        piece = (lax.shift_right_logical(words[word], shift) & ((1 << bits) - 1)) << low
        code = codes[WORDS + j]
        codes[WORDS + j] = piece if code is None else code | piece
    parts = []
    for side in range(2):
        top = ((lax.shift_right_logical(powers, 8 * side) & 0xFF) - 128).astype(F32)
        code = jnp.concatenate(codes[side * GROUPS // 2 : (side + 1) * GROUPS // 2], axis=0)
        level = code & LEVELS
        size_of = jnp.exp2(level.astype(F32) * (RANGE / LEVELS) + (top - RANGE))
        size_of = jnp.where(level == 0, 0.0, size_of)
        parts.append(jnp.where(code > LEVELS, -size_of, size_of))
    return jnp.concatenate(parts, axis=0)


def total_of(refs, starts, block, blocks, rows):
    value = None
    for ref, start in zip(refs, starts):
        term = decode(ref, block, blocks, rows) if start is None else ref[start + block]
        value = term if value is None else value + term
    return value


def merge_kernel(starts, blocks, rows, stay, *refs):
    ins, outs = refs[: len(starts)], refs[len(starts) :]
    size = blocks // len(outs)
    for p, out in enumerate(outs):

        def step(i, _):
            value = total_of(ins, starts, p * size + i, blocks, rows)
            if stay and p == 0:
                out[i] = value
            else:
                encode(out, i, size, value)
            return 0

        lax.fori_loop(0, size, step, 0, unroll=blocks <= 8)


def merge(parts, starts, blocks, pieces, stay=True):
    rows = parts[0].shape[1]
    size = blocks // pieces
    message = jax.ShapeDtypeStruct((message_rows(size, rows), LANES), jnp.int32)
    first = jax.ShapeDtypeStruct((size, rows, LANES), F32)
    shapes = [first if stay else message] + [message] * (pieces - 1)
    nbytes = 4 * blocks * rows * LANES * (len(parts) + 1)
    return pl.pallas_call(
        functools.partial(merge_kernel, starts, blocks, rows, stay),
        out_shape=shapes,
        compiler_params=room(*parts, *shapes),
        cost_estimate=pl.CostEstimate(
            flops=nbytes // 4, bytes_accessed=nbytes, transcendentals=0
        ),
        name="merge",
    )(*parts)


def rank_sums(refs, ranks):
    rows = refs[0].shape[1]
    starts = [0] + [None] * (len(refs) - 1)
    value = total_of(refs, starts, 0, 1, rows)
    product = value[: rows // 2] * value[rows // 2 :]
    return product.reshape(rows // 2 // ranks, ranks, LANES).sum(axis=1)


def partial_kernel(ranks, *refs):
    refs[-1][...] = rank_sums(refs[:-1], ranks)


def partial_scores(parts, ranks):
    queries = parts[0].shape[1] // 2 // ranks
    return pl.pallas_call(
        functools.partial(partial_kernel, ranks),
        out_shape=jax.ShapeDtypeStruct((queries, LANES), F32),
        compiler_params=room(*parts),
        name="partial_scores",
    )(*parts)


def tail_kernel(count, queries, ranks, *refs):
    ready, last = refs[:count], refs[count:-4]
    weights, doc_starts, scores, message = refs[-4:]
    parts = [ref[...] for ref in ready] + [rank_sums(last, ranks)]
    value = None
    while parts:
        chunk = []
        while sum(part.shape[0] for part in chunk) < queries:
            chunk.append(parts.pop(0))
        chunk = jnp.concatenate(chunk, axis=0)
        value = chunk if value is None else value + chunk
    value = value * weights[...]
    scores[...] = value
    lane = lax.broadcasted_iota(jnp.int32, (8, LANES), 1)
    start = jnp.where(doc_starts[...] > 0, lane, -1)
    step = 1
    while step < LANES:
        start = jnp.maximum(start, jnp.where(lane >= step, pltpu.roll(start, step, 1), -1))
        step *= 2
    start = start[0:1, :]
    lane = lane[0:1, :]
    earlier = lax.broadcasted_iota(jnp.int32, (LANES, LANES), 0)
    same_doc = ((earlier >= start) & (earlier <= lane)).astype(F32)
    total = jnp.dot(
        value, same_doc, precision=lax.Precision.HIGHEST, preferred_element_type=F32
    )
    number = (lane - jnp.maximum(start, 0) + 1).astype(F32)
    started = (start >= 0).astype(F32)
    message[0:queries, :] = total
    message[queries : queries + 1, :] = number
    message[queries + 1 : queries + 2, :] = started
    message[queries + 2 : queries + 3, :] = 1.0 - started
    message[queries + 3 :, :] = jnp.zeros_like(message[queries + 3 :, :])


def fold_members(queries, me, refs, shift):
    members = len(refs)
    tails = [ref[:, LANES - 1 : LANES] for ref in refs]
    mine = lax.rem(lax.shift_right_logical(me, shift), members)
    before = jnp.zeros_like(tails[0])
    running = jnp.zeros_like(tails[0])
    flag_row = lax.broadcasted_iota(jnp.int32, tails[0].shape, 0) == queries + 1
    for j in range(members):
        before = jnp.where(mine == j, running, before)
        value = tails[0]
        for k in range(1, members):
            value = jnp.where((mine ^ k) == j, tails[k], value)
        flag = value[queries + 1 : queries + 2, :]
        kept = jnp.where(flag > 0, value, value + running)
        running = jnp.where(flag_row, jnp.maximum(value, running), kept)
    return before, running


def group_kernel(queries, shift, me, *refs):
    before, running = fold_members(queries, me[0], refs[:-2], shift)
    refs[-2][...] = jnp.broadcast_to(before, refs[-2].shape)
    refs[-1][...] = jnp.broadcast_to(running, refs[-1].shape)


def fold_group(me, messages, queries, shift):
    shape = jax.ShapeDtypeStruct(messages[0].shape, F32)
    return pl.pallas_call(
        functools.partial(group_kernel, queries, shift),
        in_specs=[pl.BlockSpec(memory_space=pltpu.SMEM)]
        + [pl.BlockSpec(memory_space=pltpu.VMEM)] * len(messages),
        out_shape=[shape] * 2,
        compiler_params=room(),
        name="fold_group",
    )(me, *messages)


def finish_kernel(queries, shift, members, me, *refs):
    own, out = refs[-2:]
    before, _ = fold_members(queries, me[0], refs[:members], shift)
    carry = before
    for ref in refs[members:-2]:
        value = ref[:, LANES - 1 : LANES]
        flag = value[queries + 1 : queries + 2, :]
        carry = jnp.where(flag > 0, value, value + carry)
    lead = own[queries + 2 : queries + 3, :]
    total = own[0:queries, :] + lead * carry[0:queries, :]
    number = own[queries : queries + 1, :] + lead * carry[queries : queries + 1, :]
    out[...] = total / jnp.sqrt(number)


def local(
    activations, out_grads, left_factors, right_factors, token_ids, doc_starts, token_weights
):
    size, groups = lax.axis_size("loop"), lax.axis_size("groups")
    me = lax.axis_index("loop").astype(jnp.int32).reshape(1)
    rows = left_factors.shape[0]
    queries = rows * size // RANK
    part = rows // groups
    group = lax.axis_index("groups")
    depths = (left_factors.shape[1] // size, right_factors.shape[1] // size)

    def cut(factors, depth):
        mine = lax.dynamic_slice_in_dim(factors, group * part, part, axis=0)
        return mine.reshape(part, size, depth).swapaxes(0, 1)

    depth = -(-depths[1] // LANES) * LANES
    gap = jnp.zeros((size, part, depth - depths[1]), left_factors.dtype)
    outgoing = jnp.concatenate(
        [cut(right_factors, depths[1]), gap, cut(left_factors, depths[0])], axis=2
    )
    arrived = lax.all_to_all(outgoing, "loop", split_axis=0, concat_axis=0, tiled=True)
    columns = arrange(me, activations, out_grads)
    weights = jnp.take(token_weights, token_ids, mode="clip") * RANK ** (-0.5)
    arrived, columns, weights = lax.optimization_barrier((arrived, columns, weights))
    own = arrived.reshape(size * part, depth + depths[0])
    stages = later_stages(size)
    count = size // 4
    bounds = (depth, depths[1], depths[0])
    ranks = RANK // groups
    other = lax.ppermute(own, "groups", [(i, i ^ 1) for i in range(groups)])
    flows = []
    for factors, waves in zip((own, other), CHUNKS):
        if flows:
            factors, flows[-1][2] = lax.optimization_barrier((factors, flows[-1][2]))
        waves = [factors.shape[0] // w for w in waves]
        sent = project(factors, bounds, columns[: PIECES // 2], waves)
        from_core = [swap(part, "loop", 1) for part in sent]
        kept = project(factors, bounds, columns[PIECES // 2 :], waves)
        to_y = [merge([k, f], [0, 0], count, 1, stay=False)[0] for k, f in zip(kept, from_core)]
        from_y = [swap(part, "loop", 2) for part in to_y]
        flows.extend([list(flow) for flow in zip(kept, from_core, from_y)])
        if len(flows) > 1:
            flows[0][2], to_y[-1] = lax.optimization_barrier((flows[0][2], to_y[-1]))
    ready = []
    for h, values in enumerate(flows):
        if len(ready) > 1:
            values[2], ready[-2] = lax.optimization_barrier((values[2], ready[-2]))
        starts = [count, count, None]
        blocks = count
        bit = 4
        while bit < size:
            width = 4 if 2 * bit < size else 2
            pieces = merge(values, starts, blocks, width)
            offsets = (0, 2 * bit, bit, 3 * bit) if width == 4 else (0, bit)
            values = [pieces[0]] + [
                swap(piece, "loop", offset) for piece, offset in zip(pieces[1:], offsets[1:])
            ]
            blocks //= width
            starts = [0] + [None] * (width - 1)
            bit *= width
        ready.append(partial_scores(values, ranks) if h + 1 < len(flows) else values)
    last = ready.pop()

    tile = jax.ShapeDtypeStruct((queries, LANES), F32)
    scores, message = pl.pallas_call(
        functools.partial(tail_kernel, len(ready), queries, ranks),
        out_shape=[tile, jax.ShapeDtypeStruct((2 * queries, LANES), F32)],
        compiler_params=room(),
        name="tails",
    )(*ready, *last, weights[None, :], doc_starts[None, :])

    own_message = message
    befores = []
    shift = 0
    rounds = [[0, 1, 2, 3]] + stages
    for offsets in rounds[:-1]:
        messages = [message] + [swap(message, "loop", offset) for offset in offsets[1:]]
        before, message = fold_group(me, messages, queries, shift)
        befores.insert(0, before)
        shift += len(offsets).bit_length() - 1
    messages = [message] + [swap(message, "loop", offset) for offset in rounds[-1][1:]]
    influence = pl.pallas_call(
        functools.partial(finish_kernel, queries, shift, len(messages)),
        in_specs=[pl.BlockSpec(memory_space=pltpu.SMEM)]
        + [pl.BlockSpec(memory_space=pltpu.VMEM)] * (len(messages) + len(befores) + 1),
        out_shape=tile,
        compiler_params=room(),
        name="finish",
    )(me, *messages, *befores, own_message)
    return (scores.T, influence.T)


def solution(mesh):
    return jax.shard_map(
        local,
        mesh=mesh,
        in_specs=(
            P("loop", "groups"),
            P("loop", "groups"),
            P("loop", None),
            P("loop", None),
            P(("groups", "loop")),
            P(("groups", "loop")),
            P(),
        ),
        out_specs=(P(("groups", "loop"), None), P(("groups", "loop"), None)),
        check_vma=False,
    )
```

```python
import functools
import math
import jax
import jax.numpy as jnp
from jax import lax
from jax.experimental import pallas as pl
from jax.experimental.pallas import tpu as pltpu
from jax.sharding import PartitionSpec as P

RANK = 32
LANES = 128
SENT, KEPT = (6, 2), (8,)
CHUNKS = ((1,), (1,))
F32 = jnp.float32
BITS = 18
GROUPS, WORDS = 16, 9
RANGE = 24.0
LEVELS = (1 << (BITS - 1)) - 1


def swap(value, axis, offset):
    size = lax.axis_size(axis)
    return lax.ppermute(value, axis, [(i, i ^ offset) for i in range(size)])


def later_stages(size):
    stages = []
    bit = 4
    while bit < size:
        width = min(4, size // bit)
        stages.append([bit * k for k in range(width)])
        bit *= width
    return stages


def place(index, count):
    offset = 0
    bit = 1
    while bit < count:
        offset = offset * 2 + (index // bit) % 2
        bit *= 2
    return 4 * offset


def room(*arrays):
    total = sum(math.prod(a.shape) * jnp.dtype(a.dtype).itemsize for a in arrays)
    return pltpu.CompilerParams(vmem_limit_bytes=total + (4 << 20))


def arrange_kernel(me, acts, grads, *rest):
    outs, sems = rest[:-1], rest[-1]
    depth = grads.shape[0]
    half = sum(out.shape[0] for out in outs) // 2

    def copies(out, first, i):
        block = first + i
        other_core = 1 - block // half
        near = (block % half) // (half // 2)
        offset = place(block % (half // 2), half // 2) + 2 * (1 - near) + other_core
        start = pl.multiple_of((me[0] ^ offset) * LANES, LANES)
        return [
            pltpu.make_async_copy(
                ref.at[:, pl.ds(start, LANES)],
                out.at[i, pl.ds(row, ref.shape[0])],
                sems.at[k, block],
            )
            for k, (ref, row) in enumerate(((grads, 0), (acts, depth)))
        ]

    def begin(out, first, i, _):
        for copy in copies(out, first, i):
            copy.start()
        return 0

    def end(out, first, i, _):
        for copy in copies(out, first, i):
            copy.wait()
        return 0

    for step in (begin, end):
        first = 0
        for out in outs:
            lax.fori_loop(0, out.shape[0], functools.partial(step, out, first), 0)
            first += out.shape[0]


def arrange(me, acts, grads):
    blocks = acts.shape[1] // LANES
    unit = blocks // 2 // sum(SENT)
    depth = grads.shape[0] + acts.shape[0]
    shapes = [((n * unit, depth, LANES), pltpu.VMEM) for n in SENT] + [
        ((n * unit, depth, LANES), pltpu.HBM) for n in KEPT
    ]
    return pl.pallas_call(
        arrange_kernel,
        in_specs=[pl.BlockSpec(memory_space=pltpu.SMEM)]
        + [pl.BlockSpec(memory_space=pltpu.HBM)] * 2,
        out_shape=[space(shape, acts.dtype) for shape, space in shapes],
        scratch_shapes=[pltpu.SemaphoreType.DMA((2, blocks))],
        compiler_params=pltpu.CompilerParams(vmem_limit_bytes=50 << 20),
        cost_estimate=pl.CostEstimate(
            flops=0, bytes_accessed=4 * (acts.size + grads.size), transcendentals=0
        ),
        name="arrange",
    )(me, acts, grads)


def project_kernel(depths, count, factors, *rest):
    columns, outs = rest[:count], rest[count:]
    blocks = outs[0].shape[0]
    gap, right_depth, left_depth = depths

    def pair(ref, base, i, _):
        left = factors[:, gap : gap + left_depth]
        right = factors[:, 0:right_depth]
        two = range(2)
        acts = jnp.concatenate([ref[2 * i + j, right_depth:] for j in two], axis=1)
        grads = jnp.concatenate([ref[2 * i + j, :right_depth] for j in two], axis=1)
        a = jnp.dot(left, acts, preferred_element_type=F32)
        b = jnp.dot(right, grads, preferred_element_type=F32)
        first = 0
        for out in outs:
            size = out.shape[1] // 2
            for side, value in enumerate((a, b)):
                piece = value[first : first + size]
                for j in two:
                    out[base + 2 * i + j, side * size : (side + 1) * size, :] = piece[
                        :, j * LANES : (j + 1) * LANES
                    ]
            first += size
        return 0

    first = 0
    for ref in columns:
        step = functools.partial(pair, ref, first)
        lax.fori_loop(0, ref.shape[0] // 2, step, 0, unroll=blocks <= 8)
        first += ref.shape[0]


def project(factors, depths, columns, waves):
    blocks = sum(c.shape[0] for c in columns)
    shapes = [jax.ShapeDtypeStruct((blocks, 2 * w, LANES), F32) for w in waves]
    size = sum(c.size for c in columns)
    return pl.pallas_call(
        functools.partial(project_kernel, depths, len(columns)),
        out_shape=shapes,
        compiler_params=room(factors, *columns, *shapes),
        cost_estimate=pl.CostEstimate(
            flops=2 * size * factors.shape[0], bytes_accessed=2 * size, transcendentals=0
        ),
        name="project",
    )(factors, *columns)


def message_rows(blocks, rows):
    return blocks * rows // GROUPS * WORDS + -(-blocks // 8) * 8


def spread():
    spare = 32 - BITS
    places = []
    for j in range(GROUPS - WORDS):
        start = j * BITS
        while start < (j + 1) * BITS:
            word = start // spare
            end = min((j + 1) * BITS, (word + 1) * spare)
            places.append((j, word, start - j * BITS, BITS + start - word * spare, end - start))
            start = end
    return places


def encode(out, block, blocks, value):
    size = value.shape[0] // GROUPS
    half = value.shape[0] // 2
    codes, powers = [], None
    for side in range(2):
        part = value[side * half : (side + 1) * half]
        logs = jnp.log(jnp.abs(part)) * (1 / math.log(2.0))
        top = jnp.clip(jnp.ceil(jnp.max(logs, axis=0, keepdims=True)), -100.0, 100.0)
        steps = jnp.maximum((logs + (RANGE - top)) * (LEVELS / RANGE) + 0.5, 0.0)
        code = jnp.minimum(steps, float(LEVELS)).astype(jnp.int32)
        code = jnp.where(part < 0, code | (LEVELS + 1), code)
        codes.extend(code[g * size : (g + 1) * size] for g in range(GROUPS // 2))
        byte = (top.astype(jnp.int32) + 128) << (8 * side)
        powers = byte if powers is None else powers | byte
    words = codes[:WORDS]
    for j, word, low, shift, bits in spread():
        piece = lax.shift_right_logical(codes[WORDS + j], low) & ((1 << bits) - 1)
        words[word] = words[word] | (piece << shift)
    for g, word in enumerate(words):
        out[pl.ds((WORDS * block + g) * size, size), :] = word
    out[pl.ds(WORDS * blocks * size + block, 1), :] = powers


def decode(ref, block, blocks, rows):
    size = rows // GROUPS
    words = [ref[pl.ds((WORDS * block + g) * size, size), :] for g in range(WORDS)]
    powers = ref[pl.ds(WORDS * blocks * size + block, 1), :]
    codes = [word & ((1 << BITS) - 1) for word in words] + [None] * (GROUPS - WORDS)
    for j, word, low, shift, bits in spread():
        piece = (lax.shift_right_logical(words[word], shift) & ((1 << bits) - 1)) << low
        code = codes[WORDS + j]
        codes[WORDS + j] = piece if code is None else code | piece
    parts = []
    for side in range(2):
        top = ((lax.shift_right_logical(powers, 8 * side) & 0xFF) - 128).astype(F32)
        code = jnp.concatenate(codes[side * GROUPS // 2 : (side + 1) * GROUPS // 2], axis=0)
        level = code & LEVELS
        size_of = jnp.exp2(level.astype(F32) * (RANGE / LEVELS) + (top - RANGE))
        size_of = jnp.where(level == 0, 0.0, size_of)
        parts.append(jnp.where(code > LEVELS, -size_of, size_of))
    return jnp.concatenate(parts, axis=0)


def total_of(refs, starts, block, blocks, rows):
    value = None
    for ref, start in zip(refs, starts):
        term = decode(ref, block, blocks, rows) if start is None else ref[start + block]
        value = term if value is None else value + term
    return value


def merge_kernel(starts, blocks, rows, stay, *refs):
    ins, outs = refs[: len(starts)], refs[len(starts) :]
    size = blocks // len(outs)
    for p, out in enumerate(outs):

        def step(i, _):
            value = total_of(ins, starts, p * size + i, blocks, rows)
            if stay and p == 0:
                out[i] = value
            else:
                encode(out, i, size, value)
            return 0

        lax.fori_loop(0, size, step, 0, unroll=blocks <= 8)


def merge(parts, starts, blocks, pieces, stay=True):
    rows = parts[0].shape[1]
    size = blocks // pieces
    message = jax.ShapeDtypeStruct((message_rows(size, rows), LANES), jnp.int32)
    first = jax.ShapeDtypeStruct((size, rows, LANES), F32)
    shapes = [first if stay else message] + [message] * (pieces - 1)
    nbytes = 4 * blocks * rows * LANES * (len(parts) + 1)
    return pl.pallas_call(
        functools.partial(merge_kernel, starts, blocks, rows, stay),
        out_shape=shapes,
        compiler_params=room(*parts, *shapes),
        cost_estimate=pl.CostEstimate(
            flops=nbytes // 4, bytes_accessed=nbytes, transcendentals=0
        ),
        name="merge",
    )(*parts)


def rank_sums(refs, ranks):
    rows = refs[0].shape[1]
    starts = [0] + [None] * (len(refs) - 1)
    value = total_of(refs, starts, 0, 1, rows)
    product = value[: rows // 2] * value[rows // 2 :]
    return product.reshape(rows // 2 // ranks, ranks, LANES).sum(axis=1)


def partial_kernel(ranks, *refs):
    refs[-1][...] = rank_sums(refs[:-1], ranks)


def partial_scores(parts, ranks):
    queries = parts[0].shape[1] // 2 // ranks
    return pl.pallas_call(
        functools.partial(partial_kernel, ranks),
        out_shape=jax.ShapeDtypeStruct((queries, LANES), F32),
        compiler_params=room(*parts),
        name="partial_scores",
    )(*parts)


def tail_kernel(count, queries, ranks, *refs):
    ready, last = refs[:count], refs[count:-4]
    weights, doc_starts, scores, message = refs[-4:]
    parts = [ref[...] for ref in ready] + [rank_sums(last, ranks)]
    value = None
    while parts:
        chunk = []
        while sum(part.shape[0] for part in chunk) < queries:
            chunk.append(parts.pop(0))
        chunk = jnp.concatenate(chunk, axis=0)
        value = chunk if value is None else value + chunk
    value = value * weights[...]
    scores[...] = value
    lane = lax.broadcasted_iota(jnp.int32, (8, LANES), 1)
    start = jnp.where(doc_starts[...] > 0, lane, -1)
    step = 1
    while step < LANES:
        start = jnp.maximum(start, jnp.where(lane >= step, pltpu.roll(start, step, 1), -1))
        step *= 2
    start = start[0:1, :]
    lane = lane[0:1, :]
    earlier = lax.broadcasted_iota(jnp.int32, (LANES, LANES), 0)
    same_doc = ((earlier >= start) & (earlier <= lane)).astype(F32)
    total = jnp.dot(
        value, same_doc, precision=lax.Precision.HIGHEST, preferred_element_type=F32
    )
    number = (lane - jnp.maximum(start, 0) + 1).astype(F32)
    started = (start >= 0).astype(F32)
    message[0:queries, :] = total
    message[queries : queries + 1, :] = number
    message[queries + 1 : queries + 2, :] = started
    message[queries + 2 : queries + 3, :] = 1.0 - started
    message[queries + 3 :, :] = jnp.zeros_like(message[queries + 3 :, :])


def fold_members(queries, me, refs, shift):
    members = len(refs)
    tails = [ref[:, LANES - 1 : LANES] for ref in refs]
    mine = lax.rem(lax.shift_right_logical(me, shift), members)
    before = jnp.zeros_like(tails[0])
    running = jnp.zeros_like(tails[0])
    flag_row = lax.broadcasted_iota(jnp.int32, tails[0].shape, 0) == queries + 1
    for j in range(members):
        before = jnp.where(mine == j, running, before)
        value = tails[0]
        for k in range(1, members):
            value = jnp.where((mine ^ k) == j, tails[k], value)
        flag = value[queries + 1 : queries + 2, :]
        kept = jnp.where(flag > 0, value, value + running)
        running = jnp.where(flag_row, jnp.maximum(value, running), kept)
    return before, running


def group_kernel(queries, shift, me, *refs):
    before, running = fold_members(queries, me[0], refs[:-2], shift)
    refs[-2][...] = jnp.broadcast_to(before, refs[-2].shape)
    refs[-1][...] = jnp.broadcast_to(running, refs[-1].shape)


def fold_group(me, messages, queries, shift):
    shape = jax.ShapeDtypeStruct(messages[0].shape, F32)
    return pl.pallas_call(
        functools.partial(group_kernel, queries, shift),
        in_specs=[pl.BlockSpec(memory_space=pltpu.SMEM)]
        + [pl.BlockSpec(memory_space=pltpu.VMEM)] * len(messages),
        out_shape=[shape] * 2,
        compiler_params=room(),
        name="fold_group",
    )(me, *messages)


def finish_kernel(queries, shift, members, me, *refs):
    own, out = refs[-2:]
    before, _ = fold_members(queries, me[0], refs[:members], shift)
    carry = before
    for ref in refs[members:-2]:
        value = ref[:, LANES - 1 : LANES]
        flag = value[queries + 1 : queries + 2, :]
        carry = jnp.where(flag > 0, value, value + carry)
    lead = own[queries + 2 : queries + 3, :]
    total = own[0:queries, :] + lead * carry[0:queries, :]
    number = own[queries : queries + 1, :] + lead * carry[queries : queries + 1, :]
    out[...] = total / jnp.sqrt(number)


def local(
    activations, out_grads, left_factors, right_factors, token_ids, doc_starts, token_weights
):
    size, groups = lax.axis_size("loop"), lax.axis_size("groups")
    me = lax.axis_index("loop").astype(jnp.int32).reshape(1)
    rows = left_factors.shape[0]
    queries = rows * size // RANK
    part = rows // groups
    group = lax.axis_index("groups")
    depths = (left_factors.shape[1] // size, right_factors.shape[1] // size)

    def cut(factors, depth):
        mine = lax.dynamic_slice_in_dim(factors, group * part, part, axis=0)
        return mine.reshape(part, size, depth).swapaxes(0, 1)

    depth = -(-depths[1] // LANES) * LANES
    gap = jnp.zeros((size, part, depth - depths[1]), left_factors.dtype)
    outgoing = jnp.concatenate(
        [cut(right_factors, depths[1]), gap, cut(left_factors, depths[0])], axis=2
    )
    arrived = lax.all_to_all(outgoing, "loop", split_axis=0, concat_axis=0, tiled=True)
    columns = arrange(me, activations, out_grads)
    weights = jnp.take(token_weights, token_ids, mode="clip") * RANK ** (-0.5)
    arrived, columns, weights = lax.optimization_barrier((arrived, columns, weights))
    own = arrived.reshape(size * part, depth + depths[0])
    stages = later_stages(size)
    count = size // 4
    bounds = (depth, depths[1], depths[0])
    ranks = RANK // groups
    other = lax.ppermute(own, "groups", [(i, i ^ 1) for i in range(groups)])
    flows = []
    for factors, waves in zip((own, other), CHUNKS):
        if flows:
            factors, flows[-1][2] = lax.optimization_barrier((factors, flows[-1][2]))
        waves = [factors.shape[0] // w for w in waves]
        sent = project(factors, bounds, columns[: len(SENT)], waves)
        from_core = [swap(part, "loop", 1) for part in sent]
        kept = project(factors, bounds, columns[len(SENT) :], waves)
        to_y = [merge([k, f], [0, 0], count, 1, stay=False)[0] for k, f in zip(kept, from_core)]
        from_y = [swap(part, "loop", 2) for part in to_y]
        flows.extend([list(flow) for flow in zip(kept, from_core, from_y)])
        if len(flows) > 1:
            flows[0][2], to_y[-1] = lax.optimization_barrier((flows[0][2], to_y[-1]))
    ready = []
    for h, values in enumerate(flows):
        if len(ready) > 1:
            values[2], ready[-2] = lax.optimization_barrier((values[2], ready[-2]))
        starts = [count, count, None]
        blocks = count
        bit = 4
        while bit < size:
            width = 4 if 2 * bit < size else 2
            pieces = merge(values, starts, blocks, width)
            offsets = (0, 2 * bit, bit, 3 * bit) if width == 4 else (0, bit)
            values = [pieces[0]] + [
                swap(piece, "loop", offset) for piece, offset in zip(pieces[1:], offsets[1:])
            ]
            blocks //= width
            starts = [0] + [None] * (width - 1)
            bit *= width
        ready.append(partial_scores(values, ranks) if h + 1 < len(flows) else values)
    last = ready.pop()

    tile = jax.ShapeDtypeStruct((queries, LANES), F32)
    scores, message = pl.pallas_call(
        functools.partial(tail_kernel, len(ready), queries, ranks),
        out_shape=[tile, jax.ShapeDtypeStruct((2 * queries, LANES), F32)],
        compiler_params=room(),
        name="tails",
    )(*ready, *last, weights[None, :], doc_starts[None, :])

    own_message = message
    befores = []
    shift = 0
    rounds = [[0, 1, 2, 3]] + stages
    for offsets in rounds[:-1]:
        messages = [message] + [swap(message, "loop", offset) for offset in offsets[1:]]
        before, message = fold_group(me, messages, queries, shift)
        befores.insert(0, before)
        shift += len(offsets).bit_length() - 1
    messages = [message] + [swap(message, "loop", offset) for offset in rounds[-1][1:]]
    influence = pl.pallas_call(
        functools.partial(finish_kernel, queries, shift, len(messages)),
        in_specs=[pl.BlockSpec(memory_space=pltpu.SMEM)]
        + [pl.BlockSpec(memory_space=pltpu.VMEM)] * (len(messages) + len(befores) + 1),
        out_shape=tile,
        compiler_params=room(),
        name="finish",
    )(me, *messages, *befores, own_message)
    return (scores.T, influence.T)


def solution(mesh):
    return jax.shard_map(
        local,
        mesh=mesh,
        in_specs=(
            P("loop", "groups"),
            P("loop", "groups"),
            P("loop", None),
            P("loop", None),
            P(("groups", "loop")),
            P(("groups", "loop")),
            P(),
        ),
        out_specs=(P(("groups", "loop"), None), P(("groups", "loop"), None)),
        check_vma=False,
    )
```

```python
import functools
import math
import jax
import jax.numpy as jnp
from jax import lax
from jax.experimental import pallas as pl
from jax.experimental.pallas import tpu as pltpu
from jax.sharding import PartitionSpec as P

RANK = 32
LANES = 128
SENT, KEPT = (4, 2, 2), (4, 4)
CHUNKS = ((1,), (1,))
F32 = jnp.float32
BITS = 18
GROUPS, WORDS = 16, 9
RANGE = 24.0
LEVELS = (1 << (BITS - 1)) - 1


def swap(value, axis, offset):
    size = lax.axis_size(axis)
    return lax.ppermute(value, axis, [(i, i ^ offset) for i in range(size)])


def later_stages(size):
    stages = []
    bit = 4
    while bit < size:
        width = min(4, size // bit)
        stages.append([bit * k for k in range(width)])
        bit *= width
    return stages


def place(index, count):
    offset = 0
    bit = 1
    while bit < count:
        offset = offset * 2 + (index // bit) % 2
        bit *= 2
    return 4 * offset


def room(*arrays):
    total = sum(math.prod(a.shape) * jnp.dtype(a.dtype).itemsize for a in arrays)
    return pltpu.CompilerParams(vmem_limit_bytes=total + (4 << 20))


def arrange_kernel(me, acts, grads, *rest):
    outs, sems = rest[:-1], rest[-1]
    depth = grads.shape[0]
    half = sum(out.shape[0] for out in outs) // 2

    def copies(out, first, i):
        block = first + i
        other_core = 1 - block // half
        near = (block % half) // (half // 2)
        offset = place(block % (half // 2), half // 2) + 2 * (1 - near) + other_core
        start = pl.multiple_of((me[0] ^ offset) * LANES, LANES)
        return [
            pltpu.make_async_copy(
                ref.at[:, pl.ds(start, LANES)],
                out.at[i, pl.ds(row, ref.shape[0])],
                sems.at[k, block],
            )
            for k, (ref, row) in enumerate(((grads, 0), (acts, depth)))
        ]

    def begin(out, first, i, _):
        for copy in copies(out, first, i):
            copy.start()
        return 0

    def end(out, first, i, _):
        for copy in copies(out, first, i):
            copy.wait()
        return 0

    for step in (begin, end):
        first = 0
        for out in outs:
            lax.fori_loop(0, out.shape[0], functools.partial(step, out, first), 0)
            first += out.shape[0]


def arrange(me, acts, grads):
    blocks = acts.shape[1] // LANES
    unit = blocks // 2 // sum(SENT)
    depth = grads.shape[0] + acts.shape[0]
    shapes = [((n * unit, depth, LANES), pltpu.VMEM) for n in SENT] + [
        ((n * unit, depth, LANES), pltpu.HBM) for n in KEPT
    ]
    return pl.pallas_call(
        arrange_kernel,
        in_specs=[pl.BlockSpec(memory_space=pltpu.SMEM)]
        + [pl.BlockSpec(memory_space=pltpu.HBM)] * 2,
        out_shape=[space(shape, acts.dtype) for shape, space in shapes],
        scratch_shapes=[pltpu.SemaphoreType.DMA((2, blocks))],
        compiler_params=pltpu.CompilerParams(vmem_limit_bytes=50 << 20),
        cost_estimate=pl.CostEstimate(
            flops=0, bytes_accessed=4 * (acts.size + grads.size), transcendentals=0
        ),
        name="arrange",
    )(me, acts, grads)


def project_kernel(depths, count, factors, *rest):
    columns, outs = rest[:count], rest[count:]
    blocks = outs[0].shape[0]
    gap, right_depth, left_depth = depths

    def pair(ref, base, i, _):
        left = factors[:, gap : gap + left_depth]
        right = factors[:, 0:right_depth]
        two = range(2)
        acts = jnp.concatenate([ref[2 * i + j, right_depth:] for j in two], axis=1)
        grads = jnp.concatenate([ref[2 * i + j, :right_depth] for j in two], axis=1)
        a = jnp.dot(left, acts, preferred_element_type=F32)
        b = jnp.dot(right, grads, preferred_element_type=F32)
        first = 0
        for out in outs:
            size = out.shape[1] // 2
            for side, value in enumerate((a, b)):
                piece = value[first : first + size]
                for j in two:
                    out[base + 2 * i + j, side * size : (side + 1) * size, :] = piece[
                        :, j * LANES : (j + 1) * LANES
                    ]
            first += size
        return 0

    first = 0
    for ref in columns:
        step = functools.partial(pair, ref, first)
        lax.fori_loop(0, ref.shape[0] // 2, step, 0, unroll=blocks <= 8)
        first += ref.shape[0]


def project(factors, depths, columns, waves):
    blocks = sum(c.shape[0] for c in columns)
    shapes = [jax.ShapeDtypeStruct((blocks, 2 * w, LANES), F32) for w in waves]
    size = sum(c.size for c in columns)
    return pl.pallas_call(
        functools.partial(project_kernel, depths, len(columns)),
        out_shape=shapes,
        compiler_params=room(factors, *columns, *shapes),
        cost_estimate=pl.CostEstimate(
            flops=2 * size * factors.shape[0], bytes_accessed=2 * size, transcendentals=0
        ),
        name="project",
    )(factors, *columns)


def message_rows(blocks, rows):
    return blocks * rows // GROUPS * WORDS + -(-blocks // 8) * 8


def spread():
    spare = 32 - BITS
    places = []
    for j in range(GROUPS - WORDS):
        start = j * BITS
        while start < (j + 1) * BITS:
            word = start // spare
            end = min((j + 1) * BITS, (word + 1) * spare)
            places.append((j, word, start - j * BITS, BITS + start - word * spare, end - start))
            start = end
    return places


def encode(out, block, blocks, value):
    size = value.shape[0] // GROUPS
    half = value.shape[0] // 2
    codes, powers = [], None
    for side in range(2):
        part = value[side * half : (side + 1) * half]
        logs = jnp.log(jnp.abs(part)) * (1 / math.log(2.0))
        top = jnp.clip(jnp.ceil(jnp.max(logs, axis=0, keepdims=True)), -100.0, 100.0)
        steps = jnp.maximum((logs + (RANGE - top)) * (LEVELS / RANGE) + 0.5, 0.0)
        code = jnp.minimum(steps, float(LEVELS)).astype(jnp.int32)
        code = jnp.where(part < 0, code | (LEVELS + 1), code)
        codes.extend(code[g * size : (g + 1) * size] for g in range(GROUPS // 2))
        byte = (top.astype(jnp.int32) + 128) << (8 * side)
        powers = byte if powers is None else powers | byte
    words = codes[:WORDS]
    for j, word, low, shift, bits in spread():
        piece = lax.shift_right_logical(codes[WORDS + j], low) & ((1 << bits) - 1)
        words[word] = words[word] | (piece << shift)
    for g, word in enumerate(words):
        out[pl.ds((WORDS * block + g) * size, size), :] = word
    out[pl.ds(WORDS * blocks * size + block, 1), :] = powers


def decode(ref, block, blocks, rows):
    size = rows // GROUPS
    words = [ref[pl.ds((WORDS * block + g) * size, size), :] for g in range(WORDS)]
    powers = ref[pl.ds(WORDS * blocks * size + block, 1), :]
    codes = [word & ((1 << BITS) - 1) for word in words] + [None] * (GROUPS - WORDS)
    for j, word, low, shift, bits in spread():
        piece = (lax.shift_right_logical(words[word], shift) & ((1 << bits) - 1)) << low
        code = codes[WORDS + j]
        codes[WORDS + j] = piece if code is None else code | piece
    parts = []
    for side in range(2):
        top = ((lax.shift_right_logical(powers, 8 * side) & 0xFF) - 128).astype(F32)
        code = jnp.concatenate(codes[side * GROUPS // 2 : (side + 1) * GROUPS // 2], axis=0)
        level = code & LEVELS
        size_of = jnp.exp2(level.astype(F32) * (RANGE / LEVELS) + (top - RANGE))
        size_of = jnp.where(level == 0, 0.0, size_of)
        parts.append(jnp.where(code > LEVELS, -size_of, size_of))
    return jnp.concatenate(parts, axis=0)


def total_of(refs, starts, block, blocks, rows):
    value = None
    for ref, start in zip(refs, starts):
        term = decode(ref, block, blocks, rows) if start is None else ref[start + block]
        value = term if value is None else value + term
    return value


def merge_kernel(starts, blocks, rows, stay, *refs):
    ins, outs = refs[: len(starts)], refs[len(starts) :]
    size = blocks // len(outs)
    for p, out in enumerate(outs):

        def step(i, _):
            value = total_of(ins, starts, p * size + i, blocks, rows)
            if stay and p == 0:
                out[i] = value
            else:
                encode(out, i, size, value)
            return 0

        lax.fori_loop(0, size, step, 0, unroll=blocks <= 8)


def merge(parts, starts, blocks, pieces, stay=True):
    rows = parts[0].shape[1]
    size = blocks // pieces
    message = jax.ShapeDtypeStruct((message_rows(size, rows), LANES), jnp.int32)
    first = jax.ShapeDtypeStruct((size, rows, LANES), F32)
    shapes = [first if stay else message] + [message] * (pieces - 1)
    nbytes = 4 * blocks * rows * LANES * (len(parts) + 1)
    return pl.pallas_call(
        functools.partial(merge_kernel, starts, blocks, rows, stay),
        out_shape=shapes,
        compiler_params=room(*parts, *shapes),
        cost_estimate=pl.CostEstimate(
            flops=nbytes // 4, bytes_accessed=nbytes, transcendentals=0
        ),
        name="merge",
    )(*parts)


def rank_sums(refs, ranks):
    rows = refs[0].shape[1]
    starts = [0] + [None] * (len(refs) - 1)
    value = total_of(refs, starts, 0, 1, rows)
    product = value[: rows // 2] * value[rows // 2 :]
    return product.reshape(rows // 2 // ranks, ranks, LANES).sum(axis=1)


def partial_kernel(ranks, *refs):
    refs[-1][...] = rank_sums(refs[:-1], ranks)


def partial_scores(parts, ranks):
    queries = parts[0].shape[1] // 2 // ranks
    return pl.pallas_call(
        functools.partial(partial_kernel, ranks),
        out_shape=jax.ShapeDtypeStruct((queries, LANES), F32),
        compiler_params=room(*parts),
        name="partial_scores",
    )(*parts)


def tail_kernel(count, queries, ranks, *refs):
    ready, last = refs[:count], refs[count:-4]
    weights, doc_starts, scores, message = refs[-4:]
    parts = [ref[...] for ref in ready] + [rank_sums(last, ranks)]
    value = None
    while parts:
        chunk = []
        while sum(part.shape[0] for part in chunk) < queries:
            chunk.append(parts.pop(0))
        chunk = jnp.concatenate(chunk, axis=0)
        value = chunk if value is None else value + chunk
    value = value * weights[...]
    scores[...] = value
    lane = lax.broadcasted_iota(jnp.int32, (8, LANES), 1)
    start = jnp.where(doc_starts[...] > 0, lane, -1)
    step = 1
    while step < LANES:
        start = jnp.maximum(start, jnp.where(lane >= step, pltpu.roll(start, step, 1), -1))
        step *= 2
    start = start[0:1, :]
    lane = lane[0:1, :]
    earlier = lax.broadcasted_iota(jnp.int32, (LANES, LANES), 0)
    same_doc = ((earlier >= start) & (earlier <= lane)).astype(F32)
    total = jnp.dot(
        value, same_doc, precision=lax.Precision.HIGHEST, preferred_element_type=F32
    )
    number = (lane - jnp.maximum(start, 0) + 1).astype(F32)
    started = (start >= 0).astype(F32)
    message[0:queries, :] = total
    message[queries : queries + 1, :] = number
    message[queries + 1 : queries + 2, :] = started
    message[queries + 2 : queries + 3, :] = 1.0 - started
    message[queries + 3 :, :] = jnp.zeros_like(message[queries + 3 :, :])


def fold_members(queries, me, refs, shift):
    members = len(refs)
    refs = [refs[0], *refs[:0:-1]]
    tails = [ref[:, LANES - 1 : LANES] for ref in refs]
    mine = lax.rem(lax.shift_right_logical(me, shift), members)
    before = jnp.zeros_like(tails[0])
    running = jnp.zeros_like(tails[0])
    flag_row = lax.broadcasted_iota(jnp.int32, tails[0].shape, 0) == queries + 1
    for j in range(members):
        before = jnp.where(mine == j, running, before)
        value = tails[0]
        for k in range(1, members):
            value = jnp.where((mine ^ k) == j, tails[k], value)
        flag = value[queries + 1 : queries + 2, :]
        kept = jnp.where(flag > 0, value, value + running)
        running = jnp.where(flag_row, jnp.maximum(value, running), kept)
    return before, running


def group_kernel(queries, shift, me, *refs):
    before, running = fold_members(queries, me[0], refs[:-2], shift)
    refs[-2][...] = jnp.broadcast_to(before, refs[-2].shape)
    refs[-1][...] = jnp.broadcast_to(running, refs[-1].shape)


def fold_group(me, messages, queries, shift):
    shape = jax.ShapeDtypeStruct(messages[0].shape, F32)
    return pl.pallas_call(
        functools.partial(group_kernel, queries, shift),
        in_specs=[pl.BlockSpec(memory_space=pltpu.SMEM)]
        + [pl.BlockSpec(memory_space=pltpu.VMEM)] * len(messages),
        out_shape=[shape] * 2,
        compiler_params=room(),
        name="fold_group",
    )(me, *messages)


def finish_kernel(queries, shift, members, me, *refs):
    own, out = refs[-2:]
    before, _ = fold_members(queries, me[0], refs[:members], shift)
    carry = before
    for ref in refs[members:-2]:
        value = ref[:, LANES - 1 : LANES]
        flag = value[queries + 1 : queries + 2, :]
        carry = jnp.where(flag > 0, value, value + carry)
    lead = own[queries + 2 : queries + 3, :]
    total = own[0:queries, :] + lead * carry[0:queries, :]
    number = own[queries : queries + 1, :] + lead * carry[queries : queries + 1, :]
    out[...] = total / jnp.sqrt(number)


def local(
    activations, out_grads, left_factors, right_factors, token_ids, doc_starts, token_weights
):
    size, groups = lax.axis_size("loop"), lax.axis_size("groups")
    me = lax.axis_index("loop").astype(jnp.int32).reshape(1)
    rows = left_factors.shape[0]
    queries = rows * size // RANK
    part = rows // groups
    group = lax.axis_index("groups")
    depths = (left_factors.shape[1] // size, right_factors.shape[1] // size)

    def cut(factors, depth):
        mine = lax.dynamic_slice_in_dim(factors, group * part, part, axis=0)
        return mine.reshape(part, size, depth).swapaxes(0, 1)

    depth = -(-depths[1] // LANES) * LANES
    gap = jnp.zeros((size, part, depth - depths[1]), left_factors.dtype)
    outgoing = jnp.concatenate(
        [cut(right_factors, depths[1]), gap, cut(left_factors, depths[0])], axis=2
    )
    arrived = lax.all_to_all(outgoing, "loop", split_axis=0, concat_axis=0, tiled=True)
    columns = arrange(me, activations, out_grads)
    weights = jnp.take(token_weights, token_ids, mode="clip") * RANK ** (-0.5)
    arrived, columns, weights = lax.optimization_barrier((arrived, columns, weights))
    own = arrived.reshape(size * part, depth + depths[0])
    stages = later_stages(size)
    count = size // 4
    bounds = (depth, depths[1], depths[0])
    ranks = RANK // groups
    other = lax.ppermute(own, "groups", [(i, i ^ 1) for i in range(groups)])
    flows = []
    kinds = [columns[: len(SENT)], columns[len(SENT) :]]
    for factors, waves in zip((own, other), CHUNKS):
        waves = [factors.shape[0] // w for w in waves]
        if not flows:
            far = [swap(part, "loop", 1) for part in project(factors, bounds, kinds[0], waves)]
            kept = project(factors, bounds, kinds[1], waves)
            to_y = [merge([k, f], [0, 0], count, 1, stay=False)[0] for k, f in zip(kept, far)]
            from_y = [swap(part, "loop", 2) for part in to_y]
            flows.extend([k, f, y, count] for k, f, y in zip(kept, far, from_y))
            continue
        factors, flows[-1][2] = lax.optimization_barrier((factors, flows[-1][2]))
        far = [swap(part, "loop", 1) for part in project(factors, bounds, kinds[0][:1], waves)]
        kept = project(factors, bounds, kinds[1][:1], waves)
        to_y = [merge([k, f], [0, 0], count, 1, stay=False)[0] for k, f in zip(kept, far)]
        from_y = [swap(part, "loop", 2) for part in to_y]
        pass
        near = [swap(part, "loop", 1) for part in project(factors, bounds, kinds[0][1:], waves)]
        kept = project(factors, bounds, kinds[1][1:], waves)
        flows.extend([k, f, y, 0] for k, f, y in zip(kept, near, from_y))
        flows[0][2], to_y[-1] = lax.optimization_barrier((flows[0][2], to_y[-1]))
    ready = []
    for h, (*values, start) in enumerate(flows):
        if len(ready) > 1:
            values[2], ready[-2] = lax.optimization_barrier((values[2], ready[-2]))
        starts = [start, start, None]
        blocks = count
        bit = 4
        while bit < size:
            width = 4 if 2 * bit < size else 2
            pieces = merge(values, starts, blocks, width)
            offsets = (0, 2 * bit, bit, 3 * bit) if width == 4 else (0, bit)
            order = (3, 1, 2) if width == 4 else (1,)
            values = [pieces[0]] + [swap(pieces[k], "loop", offsets[k]) for k in order]
            blocks //= width
            starts = [0] + [None] * (width - 1)
            bit *= width
        ready.append(partial_scores(values, ranks) if h + 1 < len(flows) else values)
    last = ready.pop()

    tile = jax.ShapeDtypeStruct((queries, LANES), F32)
    scores, message = pl.pallas_call(
        functools.partial(tail_kernel, len(ready), queries, ranks),
        out_shape=[tile, jax.ShapeDtypeStruct((2 * queries, LANES), F32)],
        compiler_params=room(),
        name="tails",
    )(*ready, *last, weights[None, :], doc_starts[None, :])

    own_message = message
    befores = []
    shift = 0
    rounds = [[0, 1, 2, 3]] + stages
    for offsets in rounds[:-1]:
        messages = [message] + [swap(message, "loop", offset) for offset in reversed(offsets[1:])]
        before, message = fold_group(me, messages, queries, shift)
        befores.insert(0, before)
        shift += len(offsets).bit_length() - 1
    messages = [message] + [swap(message, "loop", offset) for offset in reversed(rounds[-1][1:])]
    influence = pl.pallas_call(
        functools.partial(finish_kernel, queries, shift, len(messages)),
        in_specs=[pl.BlockSpec(memory_space=pltpu.SMEM)]
        + [pl.BlockSpec(memory_space=pltpu.VMEM)] * (len(messages) + len(befores) + 1),
        out_shape=tile,
        compiler_params=room(),
        name="finish",
    )(me, *messages, *befores, own_message)
    return (scores.T, influence.T)


def solution(mesh):
    return jax.shard_map(
        local,
        mesh=mesh,
        in_specs=(
            P("loop", "groups"),
            P("loop", "groups"),
            P("loop", None),
            P("loop", None),
            P(("groups", "loop")),
            P(("groups", "loop")),
            P(),
        ),
        out_specs=(P(("groups", "loop"), None), P(("groups", "loop"), None)),
        check_vma=False,
    )
```

```python
import functools
import math
import jax
import jax.numpy as jnp
from jax import lax
from jax.experimental import pallas as pl
from jax.experimental.pallas import tpu as pltpu
from jax.sharding import PartitionSpec as P

RANK = 32
LANES = 128
SENT, KEPT = (4, 2, 2), (4, 4)
CHUNKS = ((1,), (1,))
F32 = jnp.float32
BITS = 18
GROUPS, WORDS = 16, 9
RANGE = 24.0
LEVELS = (1 << (BITS - 1)) - 1


def swap(value, axis, offset):
    size = lax.axis_size(axis)
    return lax.ppermute(value, axis, [(i, i ^ offset) for i in range(size)])


def later_stages(size):
    stages = []
    bit = 4
    while bit < size:
        width = min(4, size // bit)
        stages.append([bit * k for k in range(width)])
        bit *= width
    return stages


def place(index, count):
    offset = 0
    bit = 1
    while bit < count:
        offset = offset * 2 + (index // bit) % 2
        bit *= 2
    return 4 * offset


def room(*arrays):
    total = sum(math.prod(a.shape) * jnp.dtype(a.dtype).itemsize for a in arrays)
    return pltpu.CompilerParams(vmem_limit_bytes=total + (4 << 20))


def arrange_kernel(me, acts, grads, *rest):
    outs, sems = rest[:-1], rest[-1]
    depth = grads.shape[0]
    half = sum(out.shape[0] for out in outs) // 2

    def copies(out, first, i):
        block = first + i
        other_core = 1 - block // half
        near = (block % half) // (half // 2)
        offset = place(block % (half // 2), half // 2) + 2 * (1 - near) + other_core
        start = pl.multiple_of((me[0] ^ offset) * LANES, LANES)
        return [
            pltpu.make_async_copy(
                ref.at[:, pl.ds(start, LANES)],
                out.at[i, pl.ds(row, ref.shape[0])],
                sems.at[k, block],
            )
            for k, (ref, row) in enumerate(((grads, 0), (acts, depth)))
        ]

    def begin(out, first, i, _):
        for copy in copies(out, first, i):
            copy.start()
        return 0

    def end(out, first, i, _):
        for copy in copies(out, first, i):
            copy.wait()
        return 0

    for step in (begin, end):
        first = 0
        for out in outs:
            lax.fori_loop(0, out.shape[0], functools.partial(step, out, first), 0)
            first += out.shape[0]


def arrange(me, acts, grads):
    blocks = acts.shape[1] // LANES
    unit = blocks // 2 // sum(SENT)
    depth = grads.shape[0] + acts.shape[0]
    shapes = [((n * unit, depth, LANES), pltpu.VMEM) for n in SENT] + [
        ((n * unit, depth, LANES), pltpu.HBM) for n in KEPT
    ]
    return pl.pallas_call(
        arrange_kernel,
        in_specs=[pl.BlockSpec(memory_space=pltpu.SMEM)]
        + [pl.BlockSpec(memory_space=pltpu.HBM)] * 2,
        out_shape=[space(shape, acts.dtype) for shape, space in shapes],
        scratch_shapes=[pltpu.SemaphoreType.DMA((2, blocks))],
        compiler_params=pltpu.CompilerParams(vmem_limit_bytes=50 << 20),
        cost_estimate=pl.CostEstimate(
            flops=0, bytes_accessed=4 * (acts.size + grads.size), transcendentals=0
        ),
        name="arrange",
    )(me, acts, grads)


def project_kernel(depths, count, factors, *rest):
    columns, outs = rest[:count], rest[count:]
    blocks = outs[0].shape[0]
    gap, right_depth, left_depth = depths

    def pair(ref, base, i, _):
        left = factors[:, gap : gap + left_depth]
        right = factors[:, 0:right_depth]
        two = range(2)
        acts = jnp.concatenate([ref[2 * i + j, right_depth:] for j in two], axis=1)
        grads = jnp.concatenate([ref[2 * i + j, :right_depth] for j in two], axis=1)
        a = jnp.dot(left, acts, preferred_element_type=F32)
        b = jnp.dot(right, grads, preferred_element_type=F32)
        first = 0
        for out in outs:
            size = out.shape[1] // 2
            for side, value in enumerate((a, b)):
                piece = value[first : first + size]
                for j in two:
                    out[base + 2 * i + j, side * size : (side + 1) * size, :] = piece[
                        :, j * LANES : (j + 1) * LANES
                    ]
            first += size
        return 0

    first = 0
    for ref in columns:
        step = functools.partial(pair, ref, first)
        lax.fori_loop(0, ref.shape[0] // 2, step, 0, unroll=blocks <= 8)
        first += ref.shape[0]


def project(factors, depths, columns, waves):
    blocks = sum(c.shape[0] for c in columns)
    shapes = [jax.ShapeDtypeStruct((blocks, 2 * w, LANES), F32) for w in waves]
    size = sum(c.size for c in columns)
    return pl.pallas_call(
        functools.partial(project_kernel, depths, len(columns)),
        out_shape=shapes,
        compiler_params=room(factors, *columns, *shapes),
        cost_estimate=pl.CostEstimate(
            flops=2 * size * factors.shape[0], bytes_accessed=2 * size, transcendentals=0
        ),
        name="project",
    )(factors, *columns)


def message_rows(blocks, rows):
    return blocks * rows // GROUPS * WORDS + -(-blocks // 8) * 8


def spread():
    spare = 32 - BITS
    places = []
    for j in range(GROUPS - WORDS):
        start = j * BITS
        while start < (j + 1) * BITS:
            word = start // spare
            end = min((j + 1) * BITS, (word + 1) * spare)
            places.append((j, word, start - j * BITS, BITS + start - word * spare, end - start))
            start = end
    return places


def encode(out, block, blocks, value):
    size = value.shape[0] // GROUPS
    half = value.shape[0] // 2
    codes, powers = [], None
    for side in range(2):
        part = value[side * half : (side + 1) * half]
        logs = jnp.log(jnp.abs(part)) * (1 / math.log(2.0))
        top = jnp.clip(jnp.ceil(jnp.max(logs, axis=0, keepdims=True)), -100.0, 100.0)
        steps = jnp.maximum((logs + (RANGE - top)) * (LEVELS / RANGE) + 0.5, 0.0)
        code = jnp.minimum(steps, float(LEVELS)).astype(jnp.int32)
        code = jnp.where(part < 0, code | (LEVELS + 1), code)
        codes.extend(code[g * size : (g + 1) * size] for g in range(GROUPS // 2))
        byte = (top.astype(jnp.int32) + 128) << (8 * side)
        powers = byte if powers is None else powers | byte
    words = codes[:WORDS]
    for j, word, low, shift, bits in spread():
        piece = lax.shift_right_logical(codes[WORDS + j], low) & ((1 << bits) - 1)
        words[word] = words[word] | (piece << shift)
    for g, word in enumerate(words):
        out[pl.ds((WORDS * block + g) * size, size), :] = word
    out[pl.ds(WORDS * blocks * size + block, 1), :] = powers


def decode(ref, block, blocks, rows):
    size = rows // GROUPS
    words = [ref[pl.ds((WORDS * block + g) * size, size), :] for g in range(WORDS)]
    powers = ref[pl.ds(WORDS * blocks * size + block, 1), :]
    codes = [word & ((1 << BITS) - 1) for word in words] + [None] * (GROUPS - WORDS)
    for j, word, low, shift, bits in spread():
        piece = (lax.shift_right_logical(words[word], shift) & ((1 << bits) - 1)) << low
        code = codes[WORDS + j]
        codes[WORDS + j] = piece if code is None else code | piece
    parts = []
    for side in range(2):
        top = ((lax.shift_right_logical(powers, 8 * side) & 0xFF) - 128).astype(F32)
        code = jnp.concatenate(codes[side * GROUPS // 2 : (side + 1) * GROUPS // 2], axis=0)
        level = code & LEVELS
        size_of = jnp.exp2(level.astype(F32) * (RANGE / LEVELS) + (top - RANGE))
        size_of = jnp.where(level == 0, 0.0, size_of)
        parts.append(jnp.where(code > LEVELS, -size_of, size_of))
    return jnp.concatenate(parts, axis=0)


def total_of(refs, starts, block, blocks, rows):
    value = None
    for ref, start in zip(refs, starts):
        term = decode(ref, block, blocks, rows) if start is None else ref[start + block]
        value = term if value is None else value + term
    return value


def merge_kernel(starts, blocks, rows, stay, *refs):
    ins, outs = refs[: len(starts)], refs[len(starts) :]
    size = blocks // len(outs)
    for p, out in enumerate(outs):

        def step(i, _):
            value = total_of(ins, starts, p * size + i, blocks, rows)
            if stay and p == 0:
                out[i] = value
            else:
                encode(out, i, size, value)
            return 0

        lax.fori_loop(0, size, step, 0, unroll=blocks <= 8)


def merge(parts, starts, blocks, pieces, stay=True):
    rows = parts[0].shape[1]
    size = blocks // pieces
    message = jax.ShapeDtypeStruct((message_rows(size, rows), LANES), jnp.int32)
    first = jax.ShapeDtypeStruct((size, rows, LANES), F32)
    shapes = [first if stay else message] + [message] * (pieces - 1)
    nbytes = 4 * blocks * rows * LANES * (len(parts) + 1)
    return pl.pallas_call(
        functools.partial(merge_kernel, starts, blocks, rows, stay),
        out_shape=shapes,
        compiler_params=room(*parts, *shapes),
        cost_estimate=pl.CostEstimate(
            flops=nbytes // 4, bytes_accessed=nbytes, transcendentals=0
        ),
        name="merge",
    )(*parts)


def rank_sums(refs, ranks):
    rows = refs[0].shape[1]
    starts = [0] + [None] * (len(refs) - 1)
    value = total_of(refs, starts, 0, 1, rows)
    product = value[: rows // 2] * value[rows // 2 :]
    return product.reshape(rows // 2 // ranks, ranks, LANES).sum(axis=1)


def partial_kernel(ranks, *refs):
    refs[-1][...] = rank_sums(refs[:-1], ranks)


def partial_scores(parts, ranks):
    queries = parts[0].shape[1] // 2 // ranks
    return pl.pallas_call(
        functools.partial(partial_kernel, ranks),
        out_shape=jax.ShapeDtypeStruct((queries, LANES), F32),
        compiler_params=room(*parts),
        name="partial_scores",
    )(*parts)


def docs_kernel(queries, doc_starts, same_doc, info):
    lane = lax.broadcasted_iota(jnp.int32, (8, LANES), 1)
    start = jnp.where(doc_starts[...] > 0, lane, -1)
    step = 1
    while step < LANES:
        start = jnp.maximum(start, jnp.where(lane >= step, pltpu.roll(start, step, 1), -1))
        step *= 2
    start = start[0:1, :]
    lane = lane[0:1, :]
    earlier = lax.broadcasted_iota(jnp.int32, (LANES, LANES), 0)
    same_doc[...] = ((earlier >= start) & (earlier <= lane)).astype(F32)
    number = (lane - jnp.maximum(start, 0) + 1).astype(F32)
    started = (start >= 0).astype(F32)
    row = lax.broadcasted_iota(jnp.int32, (queries, LANES), 0)
    rest = jnp.where(row == 2, 1.0 - started, 0.0)
    info[...] = jnp.where(row == 0, number, jnp.where(row == 1, started, rest))


def documents(doc_starts, queries):
    return pl.pallas_call(
        functools.partial(docs_kernel, queries),
        out_shape=[
            jax.ShapeDtypeStruct((LANES, LANES), F32),
            jax.ShapeDtypeStruct((queries, LANES), F32),
        ],
        compiler_params=room(),
        name="documents",
    )(doc_starts[None, :])


def tail_kernel(count, queries, ranks, *refs):
    ready, last = refs[:count], refs[count:-5]
    weights, same_doc, info, scores, message = refs[-5:]
    parts = [ref[...] for ref in ready] + [rank_sums(last, ranks)]
    value = None
    while parts:
        chunk = []
        while sum(part.shape[0] for part in chunk) < queries:
            chunk.append(parts.pop(0))
        chunk = jnp.concatenate(chunk, axis=0)
        value = chunk if value is None else value + chunk
    value = value * weights[...]
    scores[...] = value
    message[0:queries, :] = jnp.dot(
        value, same_doc[...], precision=lax.Precision.HIGHEST, preferred_element_type=F32
    )
    message[queries:, :] = info[...]


def fold_members(queries, me, refs, shift):
    members = len(refs)
    refs = [refs[0], *refs[:0:-1]]
    tails = [ref[:, LANES - 1 : LANES] for ref in refs]
    mine = lax.rem(lax.shift_right_logical(me, shift), members)
    before = jnp.zeros_like(tails[0])
    running = jnp.zeros_like(tails[0])
    flag_row = lax.broadcasted_iota(jnp.int32, tails[0].shape, 0) == queries + 1
    for j in range(members):
        before = jnp.where(mine == j, running, before)
        value = tails[0]
        for k in range(1, members):
            value = jnp.where((mine ^ k) == j, tails[k], value)
        flag = value[queries + 1 : queries + 2, :]
        kept = jnp.where(flag > 0, value, value + running)
        running = jnp.where(flag_row, jnp.maximum(value, running), kept)
    return before, running


def group_kernel(queries, shift, me, *refs):
    before, running = fold_members(queries, me[0], refs[:-2], shift)
    refs[-2][...] = jnp.broadcast_to(before, refs[-2].shape)
    refs[-1][...] = jnp.broadcast_to(running, refs[-1].shape)


def fold_group(me, messages, queries, shift):
    shape = jax.ShapeDtypeStruct(messages[0].shape, F32)
    return pl.pallas_call(
        functools.partial(group_kernel, queries, shift),
        in_specs=[pl.BlockSpec(memory_space=pltpu.SMEM)]
        + [pl.BlockSpec(memory_space=pltpu.VMEM)] * len(messages),
        out_shape=[shape] * 2,
        compiler_params=room(),
        name="fold_group",
    )(me, *messages)


def finish_kernel(queries, shift, members, me, *refs):
    own, out = refs[-2:]
    before, _ = fold_members(queries, me[0], refs[:members], shift)
    carry = before
    for ref in refs[members:-2]:
        value = ref[:, LANES - 1 : LANES]
        flag = value[queries + 1 : queries + 2, :]
        carry = jnp.where(flag > 0, value, value + carry)
    lead = own[queries + 2 : queries + 3, :]
    total = own[0:queries, :] + lead * carry[0:queries, :]
    number = own[queries : queries + 1, :] + lead * carry[queries : queries + 1, :]
    out[...] = total / jnp.sqrt(number)


def local(
    activations, out_grads, left_factors, right_factors, token_ids, doc_starts, token_weights
):
    size, groups = lax.axis_size("loop"), lax.axis_size("groups")
    me = lax.axis_index("loop").astype(jnp.int32).reshape(1)
    rows = left_factors.shape[0]
    queries = rows * size // RANK
    part = rows // groups
    group = lax.axis_index("groups")
    depths = (left_factors.shape[1] // size, right_factors.shape[1] // size)

    def cut(factors, depth):
        mine = lax.dynamic_slice_in_dim(factors, group * part, part, axis=0)
        return mine.reshape(part, size, depth).swapaxes(0, 1)

    depth = -(-depths[1] // LANES) * LANES
    gap = jnp.zeros((size, part, depth - depths[1]), left_factors.dtype)
    outgoing = jnp.concatenate(
        [cut(right_factors, depths[1]), gap, cut(left_factors, depths[0])], axis=2
    )
    arrived = lax.all_to_all(outgoing, "loop", split_axis=0, concat_axis=0, tiled=True)
    columns = arrange(me, activations, out_grads)
    weights = jnp.take(token_weights, token_ids, mode="clip") * RANK ** (-0.5)
    same_doc, info = documents(doc_starts, queries)
    arrived, columns, weights, same_doc, info = lax.optimization_barrier(
        (arrived, columns, weights, same_doc, info)
    )
    own = arrived.reshape(size * part, depth + depths[0])
    stages = later_stages(size)
    count = size // 4
    bounds = (depth, depths[1], depths[0])
    ranks = RANK // groups
    other = lax.ppermute(own, "groups", [(i, i ^ 1) for i in range(groups)])
    flows = []
    kinds = [columns[: len(SENT)], columns[len(SENT) :]]
    for factors, waves in zip((own, other), CHUNKS):
        waves = [factors.shape[0] // w for w in waves]
        if not flows:
            far = [swap(part, "loop", 1) for part in project(factors, bounds, kinds[0], waves)]
            kept = project(factors, bounds, kinds[1], waves)
            to_y = [merge([k, f], [0, 0], count, 1, stay=False)[0] for k, f in zip(kept, far)]
            from_y = [swap(part, "loop", 2) for part in to_y]
            flows.extend([k, f, y, count] for k, f, y in zip(kept, far, from_y))
            continue
        factors, flows[-1][2] = lax.optimization_barrier((factors, flows[-1][2]))
        far = [swap(part, "loop", 1) for part in project(factors, bounds, kinds[0][:1], waves)]
        kept = project(factors, bounds, kinds[1][:1], waves)
        to_y = [merge([k, f], [0, 0], count, 1, stay=False)[0] for k, f in zip(kept, far)]
        from_y = [swap(part, "loop", 2) for part in to_y]
        pass
        near = [swap(part, "loop", 1) for part in project(factors, bounds, kinds[0][1:], waves)]
        kept = project(factors, bounds, kinds[1][1:], waves)
        flows.extend([k, f, y, 0] for k, f, y in zip(kept, near, from_y))
        flows[0][2], to_y[-1] = lax.optimization_barrier((flows[0][2], to_y[-1]))
    ready = []
    for h, (*values, start) in enumerate(flows):
        if len(ready) > 1:
            values[2], ready[-2] = lax.optimization_barrier((values[2], ready[-2]))
        starts = [start, start, None]
        blocks = count
        bit = 4
        while bit < size:
            width = 4 if 2 * bit < size else 2
            pieces = merge(values, starts, blocks, width)
            offsets = (0, 2 * bit, bit, 3 * bit) if width == 4 else (0, bit)
            order = (3, 1, 2) if width == 4 else (1,)
            values = [pieces[0]] + [swap(pieces[k], "loop", offsets[k]) for k in order]
            blocks //= width
            starts = [0] + [None] * (width - 1)
            bit *= width
        ready.append(partial_scores(values, ranks) if h + 1 < len(flows) else values)
    last = ready.pop()

    tile = jax.ShapeDtypeStruct((queries, LANES), F32)
    scores, message = pl.pallas_call(
        functools.partial(tail_kernel, len(ready), queries, ranks),
        out_shape=[tile, jax.ShapeDtypeStruct((2 * queries, LANES), F32)],
        compiler_params=room(),
        name="tails",
    )(*ready, *last, weights[None, :], same_doc, info)

    own_message = message
    befores = []
    shift = 0
    rounds = [[0, 1, 2, 3]] + stages
    for offsets in rounds[:-1]:
        messages = [message] + [swap(message, "loop", offset) for offset in reversed(offsets[1:])]
        before, message = fold_group(me, messages, queries, shift)
        befores.insert(0, before)
        shift += len(offsets).bit_length() - 1
    messages = [message] + [swap(message, "loop", offset) for offset in reversed(rounds[-1][1:])]
    influence = pl.pallas_call(
        functools.partial(finish_kernel, queries, shift, len(messages)),
        in_specs=[pl.BlockSpec(memory_space=pltpu.SMEM)]
        + [pl.BlockSpec(memory_space=pltpu.VMEM)] * (len(messages) + len(befores) + 1),
        out_shape=tile,
        compiler_params=room(),
        name="finish",
    )(me, *messages, *befores, own_message)
    return (scores.T, influence.T)


def solution(mesh):
    return jax.shard_map(
        local,
        mesh=mesh,
        in_specs=(
            P("loop", "groups"),
            P("loop", "groups"),
            P("loop", None),
            P("loop", None),
            P(("groups", "loop")),
            P(("groups", "loop")),
            P(),
        ),
        out_specs=(P(("groups", "loop"), None), P(("groups", "loop"), None)),
        check_vma=False,
    )
```
